256 devices in a mesh: row: 16 (over z, core), col: 16 (over y, x).
Axes of the slice: x: 4, y: 4, z: 8, core: 2. Of those that a mesh axis runs over, the one named last changes fastest.
Arguments:
- features: bfloat16 [65536, 512], P(('col', 'row')), may hold values from -6 to 6
- tile_values: bfloat16 [16, 16, 96, 128, 128], P('row', 'col'), may hold values from -0.078125 to 0.078125
- tile_row: int32 [16, 16, 96], P('row', 'col'), may hold values from 0 to 31
- tile_col: int32 [16, 16, 96], P('row', 'col'), may hold values from 0 to 31
- tile_count: int32 [16, 16], P('row', 'col'), may hold values from 24 to 96, as said below
- weight: float32 [512, 512], replicated, may hold values from -0.25 to 0.25
- bias: float32 [512], replicated, may hold values from -3 to 3
- second_weight: float32 [512, 512], replicated, may hold values from 100 to 10000
- second_bias: float32 [512], replicated, may hold values from 100 to 10000
- cotangent: bfloat16 [65536, 512], P(('row', 'col')), may hold values from -6 to 6
Outputs:
- activations: bfloat16 [65536, 512], P(('row', 'col'))
- grad_features: bfloat16 [65536, 512], P(('col', 'row'))
- new_weight: float32 [512, 512], replicated
- new_bias: float32 [512], replicated
The draws below stay inside these ranges and needn't reach their ends.
Inputs may be any that keep to these rules, and one draw needn't show every extreme that they name: `tile_count`: every block uses at least a quarter of its 96 slots, and some block uses all of them.
All inputs are finite; a program needn't handle non-finite values.
Results may differ from the reference program's by a relative error of at most 0.0072.
Values may be sent and summed in bfloat16 or wider, within the bound.
No kernel may reach another device: no remote copies, remote signals or barrier semaphores. Data moves between devices by JAX's collectives and lax.ppermute only.
A program may use at most 128 MiB of HBM per device.

```python
import math
import jax
import jax.numpy as jnp
import numpy as np
from jax import lax

F = 512
TILE = 128
ROWS_DEV = 256
TILES_DEV = 96
ROW_TILES = 32
COL_TILES = 32
NODES = 65536
N_ROW = 16
N_COL = 16


def draw_tile_count(key, part):
    key = jax.random.fold_in(key, 7)
    first_key, second_key = jax.random.split(key)
    counts = jax.random.randint(first_key, (N_ROW * N_COL,), TILES_DEV // 4, TILES_DEV + 1)
    chosen = jax.random.randint(second_key, (), 0, N_ROW * N_COL)
    counts = jnp.where(jnp.arange(N_ROW * N_COL) == chosen, TILES_DEV, counts)
    return counts.reshape(N_ROW, N_COL).astype(jnp.int32)


def with_ends(drawn, key, least, high):
    dims = drawn.shape
    index_at = [jax.random.randint(jax.random.fold_in(key, axis), (), 0, dims[axis]) for axis in range(len(dims))]
    drawn = drawn.at[tuple(index_at)].set(least)
    longest = dims.index(max(dims))
    index_at[longest] = (index_at[longest] + 1) % dims[longest]
    return drawn.at[tuple(index_at)].set(high)


def shard_levels(rng, dims, cuts, smallest, largest):
    gain, own = 1.0, jax.random.fold_in(rng, 6)
    for position, shards_of in cuts:
        draws = jnp.exp(jax.random.uniform(jax.random.fold_in(own, position), (shards_of,), jnp.float32, smallest / len(cuts), largest / len(cuts)))
        gain = gain * jnp.repeat(draws, dims[position] // shards_of).reshape([-1 if axis == position else 1 for axis in range(len(dims))])
    return gain


def rank_table(amount, lean):
    weights = [(1 << 20) // math.isqrt(grade ** lean) + 1 for grade in range(1, amount + 1)]
    deviation = 1 + sum(weights) // (1 << 30)
    return np.cumsum(np.array([max(1, weight // deviation) for weight in weights]))


def skewed_ids(stream_key, shape, count, slope):
    table = rank_table(count, slope)
    lot = jax.random.randint(jax.random.fold_in(stream_key, 1), shape, 0, int(table[count - 1]))
    standing = jnp.searchsorted(jnp.asarray(table, jnp.int32), lot, side="right")
    return jax.random.permutation(jax.random.fold_in(stream_key, 2), count)[standing].astype(jnp.int32)


def scatter_about(key, extent, scale, bound, cuts=(), kind=jnp.bfloat16):
    values = jax.random.normal(key, extent, jnp.float32) * scale
    if len(cuts) > 0:
        values = shard_levels(key, extent, cuts, -0.22, 0.18) * values
    return jnp.clip(values, min=-bound, max=bound).astype(kind)


def setup_inputs(seed: int = 0) -> dict:
    key_list = jax.random.split(jax.random.key(seed), 11)
    features = scatter_about(key_list[0], (NODES, F), 1.0, 6.0, ((0, 256),))
    tile_values = scatter_about(key_list[1], (N_ROW, N_COL, TILES_DEV, TILE, TILE), (TILES_DEV * TILE * TILE // ROWS_DEV) ** -0.5, 0.078125, ((0, 16), (1, 16)))
    tile_row = with_ends(skewed_ids(key_list[2], (N_ROW, N_COL, TILES_DEV), ROW_TILES, 2), jax.random.fold_in(key_list[2], 3), 0, ROW_TILES - 1).astype(jnp.int32)
    tile_col = with_ends(jax.random.randint(key_list[3], (N_ROW, N_COL, TILES_DEV), 0, COL_TILES), jax.random.fold_in(key_list[3], 1), 0, COL_TILES - 1).astype(jnp.int32)
    tile_count = draw_tile_count(jax.random.fold_in(key_list[10], 71), 0)
    weight = scatter_about(key_list[5], (F, F), F ** -0.5, 0.25, (), jnp.float32)
    bias = scatter_about(key_list[6], (F,), 0.5, 3.0, (), jnp.float32)
    second_weight = jnp.clip(jnp.exp(jax.random.uniform(key_list[7], (F, F), jnp.float32, math.log(100.0), math.log(10000.0))), 100.0, 10000.0)
    second_bias = jnp.clip(jnp.exp(jax.random.uniform(key_list[8], (F,), jnp.float32, math.log(100.0), math.log(10000.0))), 100.0, 10000.0)
    cotangent = scatter_about(key_list[9], (NODES, F), 1.0, 6.0, ((0, 256),))
    return {"features": features, "tile_values": tile_values, "tile_row": tile_row, "tile_col": tile_col, "tile_count": tile_count, "weight": weight, "bias": bias, "second_weight": second_weight, "second_bias": second_bias, "cotangent": cotangent}


learn_rate = 0.1

def accumulate(values, sources, targets, valid_mask, source, out_tiles, flip):
    tile = values.shape[-1]
    width = source.shape[1]
    blocks = source.reshape(-1, tile, width)
    form = 'kji,kjf->kif' if flip else 'kij,kjf->kif'

    def device_step(running, inputs):
        tiles_now, from_now, to_now, live_now = inputs
        pieces = blocks[from_now].astype(jnp.float32) * live_now[:, None, None]
        product = jnp.einsum(form, tiles_now.astype(jnp.float32), pieces)
        return (running.at[to_now].add(product), None)
    start_value = jnp.zeros((out_tiles, tile, width), jnp.float32)
    running, unused = lax.scan(device_step, start_value, (values, sources, targets, valid_mask))
    return running.reshape(-1, width)

def refresh(param, grad, second):
    moment = 0.9 * second + 0.1 * grad * grad
    return param - learn_rate * grad / (jnp.sqrt(moment) + 1e-06)

def reference(features, tile_values, tile_row, tile_col, tile_count, weight, bias, second_weight, second_bias, cotangent):
    devices_all = N_ROW * N_COL
    slots = tile_values.shape[2]
    row_base = (jnp.arange(N_ROW, dtype=jnp.int32) * ROW_TILES)[:, None, None]
    col_base = (jnp.arange(N_COL, dtype=jnp.int32) * COL_TILES)[None, :, None]
    rows_global = (tile_row + row_base).reshape(devices_all, slots).astype(jnp.int32)
    cols_global = (tile_col + col_base).reshape(devices_all, slots).astype(jnp.int32)
    valid_mask = (jnp.arange(slots, dtype=jnp.int32)[None, None, :] < tile_count[:, :, None]).astype(jnp.float32)
    valid_mask = valid_mask.reshape(devices_all, slots)
    values = tile_values.reshape(devices_all, slots, TILE, TILE)
    aggregated = accumulate(values, cols_global, rows_global, valid_mask, features, N_ROW * ROW_TILES, False).astype(jnp.bfloat16)
    low_weight = weight.astype(jnp.bfloat16)
    pre = jnp.dot(aggregated, low_weight, preferred_element_type=jnp.float32) + bias
    sigma = jax.nn.sigmoid(pre)
    activations = (pre * sigma).astype(jnp.bfloat16)
    grad_pre = (cotangent.astype(jnp.float32) * sigma * (1.0 + pre * (1.0 - sigma))).astype(jnp.bfloat16)
    grad_weight = jnp.dot(aggregated.T, grad_pre, preferred_element_type=jnp.float32)
    grad_bias = lax.optimization_barrier(jnp.sum(grad_pre.astype(jnp.float32), axis=0))
    grad_aggregated = jnp.dot(grad_pre, low_weight.T, preferred_element_type=jnp.float32).astype(jnp.bfloat16)
    grad_features = accumulate(values, rows_global, cols_global, valid_mask, grad_aggregated, N_COL * COL_TILES, True).astype(jnp.bfloat16)
    new_weight = refresh(weight, grad_weight, second_weight)
    new_bias = refresh(bias, grad_bias, second_bias)
    return (activations, grad_features, new_weight, new_bias)
```

```python
import functools

import jax
import jax.numpy as jnp
from jax import lax
from jax.experimental import pallas as pl
from jax.experimental.pallas import tpu as pltpu
from jax.sharding import Mesh, PartitionSpec as P

learn_rate = 0.1
TILE = 128
F = 512
BLOCK_TILES = 32
UNROLL = 4
Z = 8
VMEM_BYTES = 48 * 1024 * 1024


def refresh(param, grad, second):
    moment = 0.9 * second + 0.1 * grad * grad
    return param - learn_rate * grad / (jnp.sqrt(moment) + 1e-06)


def select(index, table):
    return jnp.take(jnp.array(table, jnp.int32), index)


def row_tile_parts(t):
    y, x, half = t // 8, t // 2 % 4, t % 2
    dy = (y - lax.axis_index("y")) % 4
    dx = (x - lax.axis_index("x")) % 4
    return dy, dx, half


def scatter_place(t):
    dy, dx, half = row_tile_parts(t)
    major, minor = jnp.where(half == 0, dx, dy), jnp.where(half == 0, dy, dx)
    return half * 16 + select(major, [3, 1, 0, 2]) * 4 + minor


def gather_place(t):
    dy, dx, half = row_tile_parts(t)
    major, minor = jnp.where(half == 0, dy, dx), jnp.where(half == 0, dx, dy)
    order = [0, 2, 3, 1]
    return half * 16 + select(major, order) * 4 + select(minor, order)


def col_tile_parts(t):
    z, core, half = t // 4, t // 2 % 2, t % 2
    dz = (z - lax.axis_index("z")) % Z
    return dz, (core != lax.axis_index("core")).astype(jnp.int32), half


def gather_z_place(t):
    dz, other, half = col_tile_parts(t)
    low = select(dz, [0, 3, 7, 11, 14, 10, 6, 2])
    high = select(dz, [1, 5, 9, 13, 15, 12, 8, 4])
    return other * 16 + jnp.where(half == 0, low, high)


def scatter_z_place(t):
    dz, other, half = col_tile_parts(t)
    low = select(dz, [14, 12, 8, 4, 0, 2, 6, 10])
    high = select(dz, [15, 11, 7, 3, 1, 5, 9, 13])
    return other * 16 + jnp.where(half == 0, low, high)


def slot_loop(count, sources, targets, values, panel, acc, flip):
    contract = ((0,), (0,)) if flip else ((1,), (0,))

    def step(group, carry):
        for part in range(UNROLL):
            k = group * UNROLL + part
            source = sources[k]
            target = jnp.where(k < count, targets[k], BLOCK_TILES)
            for column in range(0, F, 256):
                columns = slice(column, column + 256)
                acc[target, :, columns] += lax.dot_general(
                    values[k],
                    panel[source, :, columns],
                    (contract, ((), ())),
                    preferred_element_type=jnp.float32,
                )
        return carry

    lax.fori_loop(0, (count + UNROLL - 1) // UNROLL, step, 0)


def product_kernel(flip, n_panels, sources, targets, count, values_hbm, *refs):
    panels, refs = refs[:n_panels], refs[n_panels:]
    outs, (values, panel, acc, sems) = refs[:-4], refs[-4:]
    copies = [pltpu.make_async_copy(values_hbm, values, sems.at[0])]
    start = 0
    for i, piece in enumerate(panels):
        tiles = piece.shape[0]
        copies.append(pltpu.make_async_copy(piece, panel.at[pl.ds(start, tiles)], sems.at[i + 1]))
        start += tiles
    for copy in copies:
        copy.start()
    acc[...] = jnp.zeros_like(acc)
    for copy in copies:
        copy.wait()
    slot_loop(count[0], sources, targets, values, panel, acc, flip)
    start = 0
    for out in outs:
        for t in range(out.shape[0]):
            out[t] = acc[start + t].astype(jnp.bfloat16)
        start += out.shape[0]


def product_call(flip, sources, targets, count, values, panels, out_tiles):
    hbm = pl.BlockSpec(memory_space=pl.ANY)
    smem = pl.BlockSpec(memory_space=pltpu.SMEM)
    vmem = pl.BlockSpec(memory_space=pltpu.VMEM)
    slots = values.shape[0]
    return pl.pallas_call(
        functools.partial(product_kernel, flip, len(panels)),
        out_shape=[jax.ShapeDtypeStruct((n, TILE, F), jnp.bfloat16) for n in out_tiles],
        in_specs=[smem] * 3 + [hbm] * (1 + len(panels)),
        out_specs=[vmem] * len(out_tiles),
        scratch_shapes=[
            pltpu.VMEM((slots, TILE, TILE), jnp.bfloat16),
            pltpu.VMEM((BLOCK_TILES, TILE, F), jnp.bfloat16),
            pltpu.VMEM((BLOCK_TILES + 1, TILE, F), jnp.float32),
            pltpu.SemaphoreType.DMA((1 + len(panels),)),
        ],
        compiler_params=pltpu.CompilerParams(vmem_limit_bytes=VMEM_BYTES),
        cost_estimate=pl.CostEstimate(
            flops=2 * slots * TILE * TILE * F, bytes_accessed=11 * 2**20, transcendentals=0
        ),
    )(sources, targets, count, values, *panels)


def dense_kernel(
    aggregated, cotangent, low_weight, bias, activations, grad_pre, grad_first, grad_last
):
    w = low_weight[...]
    pre = jnp.dot(aggregated[...], w, preferred_element_type=jnp.float32) + bias[...]
    sigma = jax.nn.sigmoid(pre)
    grad = cotangent[...].astype(jnp.float32) * sigma * (1.0 + pre * (1.0 - sigma))
    low_grad = grad.astype(jnp.bfloat16)
    activations[...] = (pre * sigma).astype(jnp.bfloat16)
    grad_pre[...] = low_grad
    grad_aggregated = lax.dot_general(
        low_grad, w, (((1,), (1,)), ((), ())), preferred_element_type=jnp.float32
    ).astype(jnp.bfloat16)
    grad_first[...] = grad_aggregated[:TILE]
    grad_last[...] = grad_aggregated[TILE:]


def dense_call(aggregated, cotangent, low_weight, bias):
    shape = jax.ShapeDtypeStruct(aggregated.shape, jnp.bfloat16)
    half = jax.ShapeDtypeStruct((TILE, F), jnp.bfloat16)
    return pl.pallas_call(
        dense_kernel,
        out_shape=[shape, shape, half, half],
        compiler_params=pltpu.CompilerParams(vmem_limit_bytes=VMEM_BYTES),
    )(aggregated, cotangent, low_weight, bias)


def swap(value, axis, bit):
    size = lax.axis_size(axis)
    return lax.ppermute(value, axis, [(i, i ^ (1 << bit)) for i in range(size)])


def shift(value, axis, by):
    size = lax.axis_size(axis)
    return lax.ppermute(value, axis, [(i, (i + by) % size) for i in range(size)])


def wide(value):
    return value.astype(jnp.float32)


def low(value):
    return value.astype(jnp.bfloat16)


def gather_z(features):
    own = features.reshape(2, TILE, F)
    pieces = [own]
    a_right = a_left = own[0:1]
    b_right = b_left = own[1:2]
    for step in range(1, 4):
        a_right, a_left = shift(a_right, "z", 1), shift(a_left, "z", -1)
        b_right, b_left = shift(b_right, "z", 1), shift(b_left, "z", -1)
        pieces.append(jnp.concatenate([a_right, a_left, b_right, b_left], axis=0))
    a_right, b_left = shift(a_right, "z", 1), shift(b_left, "z", -1)
    pieces.append(jnp.concatenate([a_right, b_left], axis=0))
    return pieces + [swap(piece, "core", 0) for piece in pieces]


def scatter_ring(far_up, far_down, up, down, own, axis):
    from_below = shift(far_up, axis, 1)
    from_above = shift(far_down, axis, -1)
    split = far_up.shape[0]
    up_sum = jnp.concatenate([low(wide(up[:split]) + wide(from_below)), up[split:]], axis=0)
    down_sum = jnp.concatenate([down[:split], low(wide(down[split:]) + wide(from_above))], axis=0)
    below = shift(up_sum, axis, 1)
    above = shift(down_sum, axis, -1)
    return wide(own) + wide(below) + wide(above)


def scatter_xy(pieces, first, second):
    sums = scatter_ring(*pieces, first)
    own, up, far, down = (low(sums[i]) for i in range(4))
    return scatter_ring(far[: TILE // 2], far[TILE // 2 :], up, down, own, second)


def gather_ring(own, axis):
    below = shift(own, axis, 1)
    above = shift(own, axis, -1)
    half = own.shape[0] // 2
    far_first = shift(above[:half], axis, -1)
    far_last = shift(below[half:], axis, 1)
    return [own, below, above, far_first, far_last]


def gather_xy(own, first, second):
    bundle = jnp.concatenate(gather_ring(own, first), axis=0)
    return gather_ring(bundle.reshape(4, TILE, F), second)


def scatter_z(own, other):
    received = [swap(piece, "core", 0) for piece in other]

    def term(step, index):
        return wide(own[step][index]) + wide(received[step][index])

    a_right, b_left, a_left, b_right = (low(term(0, i)) for i in range(4))
    for step in range(1, 4):
        a_right, a_left = shift(a_right, "z", 1), shift(a_left, "z", -1)
        b_right, b_left = shift(b_right, "z", 1), shift(b_left, "z", -1)
        a_right = low(term(step, 0) + wide(a_right))
        b_left = low(term(step, 1) + wide(b_left))
        if step < 3:
            a_left = low(term(step, 2) + wide(a_left))
            b_right = low(term(step, 3) + wide(b_right))
    a_sum = term(3, 2) + wide(a_left) + wide(shift(a_right, "z", 1))
    b_sum = term(3, 3) + wide(b_right) + wide(shift(b_left, "z", -1))
    return low(jnp.concatenate([a_sum, b_sum], axis=0))


def sum_everywhere(total):
    side = lax.axis_index("core")
    rows = total.shape[0] // 2
    keep = lax.dynamic_slice_in_dim(total, side * rows, rows, 0)
    send = lax.dynamic_slice_in_dim(total, (1 - side) * rows, rows, 0)
    total = keep + swap(send, "core", 0)
    total = lax.psum_scatter(total, "z", scatter_dimension=0, tiled=True)
    for axis, bit in [("x", 0), ("x", 1), ("y", 0), ("y", 1)]:
        total = total + swap(total, axis, bit)
    total = lax.all_gather(total, "z", axis=0, tiled=True)
    other = swap(total, "core", 0)
    return jnp.concatenate(
        [jnp.where(side == 0, total, other), jnp.where(side == 0, other, total)], axis=0
    )


def per_device(
    features,
    tile_values,
    tile_row,
    tile_col,
    tile_count,
    weight,
    bias,
    second_weight,
    second_bias,
    cotangent,
):
    values = tile_values[0, 0]
    rows_local = tile_row[0, 0]
    cols_local = tile_col[0, 0]
    count = tile_count[0]
    low_weight = weight.astype(jnp.bfloat16)

    partials = product_call(
        False,
        gather_z_place(cols_local),
        scatter_place(rows_local),
        count,
        values,
        gather_z(features),
        [2, 2, 4, 4, 4] * 2,
    )
    sums = [scatter_xy(partials[:5], "x", "y"), scatter_xy(partials[5:], "y", "x")]
    aggregated = low(jnp.concatenate(sums, axis=0))
    activations, grad_pre, grad_first, grad_last = dense_call(
        aggregated, cotangent, low_weight, bias.reshape(1, F)
    )
    grad_panels = gather_xy(grad_first, "x", "y") + gather_xy(grad_last, "y", "x")

    with_ones = jnp.concatenate(
        [aggregated, jnp.ones((aggregated.shape[0], TILE), jnp.bfloat16)], axis=1
    )
    local_grad = lax.dot_general(
        with_ones, grad_pre, (((0,), (0,)), ((), ())), preferred_element_type=jnp.float32
    )
    total_grad = sum_everywhere(local_grad)
    new_weight = refresh(weight, total_grad[:F], second_weight)
    new_bias = refresh(bias, total_grad[F], second_bias)

    grad_partials = product_call(
        True,
        gather_place(rows_local),
        scatter_z_place(cols_local),
        count,
        values,
        grad_panels,
        [4] * 8,
    )
    grad_features = scatter_z(grad_partials[:4], grad_partials[4:])
    return (activations, grad_features, new_weight, new_bias)


def solution(mesh):
    fine = Mesh(mesh.devices.reshape(Z, 2, 4, 4), ("z", "core", "y", "x"))
    row = ("z", "core")
    col = ("y", "x")
    placed = (
        P(col + row, None),
        P(row, col, None, None, None),
        P(row, col, None),
        P(row, col, None),
        P(row, col),
        P(),
        P(),
        P(),
        P(),
        P(row + col, None),
    )
    return jax.shard_map(
        per_device,
        mesh=fine,
        in_specs=placed,
        out_specs=(P(row + col, None), P(col + row, None), P(), P()),
        check_vma=False,
    )
```

```python
import functools

import jax
import jax.numpy as jnp
from jax import lax
from jax.experimental import pallas as pl
from jax.experimental.pallas import tpu as pltpu
from jax.sharding import Mesh, PartitionSpec as P

learn_rate = 0.1
TILE = 128
F = 512
BLOCK_TILES = 32
UNROLL = 4
Z = 8
VMEM_BYTES = 48 * 1024 * 1024


def refresh(param, grad, second):
    moment = 0.9 * second + 0.1 * grad * grad
    return param - learn_rate * grad / (jnp.sqrt(moment) + 1e-06)


def select(index, table):
    return jnp.take(jnp.array(table, jnp.int32), index)


def pick(index, other, same_table, other_table):
    return jnp.where(other == 0, select(index, same_table), select(index, other_table))


def row_tile_parts(t):
    dy = (t // 8 - lax.axis_index("y")) % 4
    dx = (t // 2 % 4 - lax.axis_index("x")) % 4
    x_first = lax.axis_index("core") == 0
    return jnp.where(x_first, dx, dy), jnp.where(x_first, dy, dx), t % 2


def scatter_xy_place(t):
    first, second, half = row_tile_parts(t)
    return select(first, [3, 1, 0, 2]) * 8 + second * 2 + half


def gather_xy_place(t):
    first, second, half = row_tile_parts(t)
    order = [0, 2, 3, 1]
    return select(second, order) * 8 + select(first, order) * 2 + half


def col_tile_parts(t):
    dz = (t // 4 - lax.axis_index("z")) % Z
    core = lax.axis_index("core")
    return dz, core, (t // 2 % 2 != core).astype(jnp.int32), t % 2


def gather_z_place(t):
    dz, core, other, half = col_tile_parts(t)
    behind = jnp.where(core == 0, (Z - dz) % Z, dz)
    return pick(behind, other, [0, 4, 8, 12, 16, 28, 24, 20], [2, 6, 10, 14, 30, 26, 22, 18]) + half


def scatter_z_place(t):
    dz, core, other, half = col_tile_parts(t)
    ahead = jnp.where(core == 0, dz, (Z - dz) % Z)
    return pick(ahead, other, [14, 10, 6, 2, 0, 20, 24, 28], [30, 12, 8, 4, 16, 18, 22, 26]) + half


def slot_loop(count, sources, targets, values, panel, acc, flip):
    contract = ((0,), (0,)) if flip else ((1,), (0,))

    def step(group, carry):
        for part in range(UNROLL):
            k = group * UNROLL + part
            source = sources[k]
            target = jnp.where(k < count, targets[k], BLOCK_TILES)
            for column in range(0, F, 256):
                columns = slice(column, column + 256)
                acc[target, :, columns] += lax.dot_general(
                    values[k],
                    panel[source, :, columns],
                    (contract, ((), ())),
                    preferred_element_type=jnp.float32,
                )
        return carry

    lax.fori_loop(0, (count + UNROLL - 1) // UNROLL, step, 0)


def product_kernel(flip, n_panels, sources, targets, count, values_hbm, *refs):
    panels, refs = refs[:n_panels], refs[n_panels:]
    outs, (values, panel, acc, sems) = refs[:-4], refs[-4:]
    copies = [pltpu.make_async_copy(values_hbm, values, sems.at[0])]
    start = 0
    for i, piece in enumerate(panels):
        tiles = piece.shape[0]
        copies.append(pltpu.make_async_copy(piece, panel.at[pl.ds(start, tiles)], sems.at[i + 1]))
        start += tiles
    for copy in copies:
        copy.start()
    acc[...] = jnp.zeros_like(acc)
    for copy in copies:
        copy.wait()
    slot_loop(count[0], sources, targets, values, panel, acc, flip)
    start = 0
    for out in outs:
        for t in range(out.shape[0]):
            out[t] = acc[start + t].astype(jnp.bfloat16)
        start += out.shape[0]


def product_call(flip, sources, targets, count, values, panels, out_tiles):
    hbm = pl.BlockSpec(memory_space=pl.ANY)
    smem = pl.BlockSpec(memory_space=pltpu.SMEM)
    vmem = pl.BlockSpec(memory_space=pltpu.VMEM)
    slots = values.shape[0]
    return pl.pallas_call(
        functools.partial(product_kernel, flip, len(panels)),
        out_shape=[jax.ShapeDtypeStruct((n, TILE, F), jnp.bfloat16) for n in out_tiles],
        in_specs=[smem] * 3 + [hbm] * (1 + len(panels)),
        out_specs=[vmem] * len(out_tiles),
        scratch_shapes=[
            pltpu.VMEM((slots, TILE, TILE), jnp.bfloat16),
            pltpu.VMEM((BLOCK_TILES, TILE, F), jnp.bfloat16),
            pltpu.VMEM((BLOCK_TILES + 1, TILE, F), jnp.float32),
            pltpu.SemaphoreType.DMA((1 + len(panels),)),
        ],
        compiler_params=pltpu.CompilerParams(vmem_limit_bytes=VMEM_BYTES),
        cost_estimate=pl.CostEstimate(
            flops=2 * slots * TILE * TILE * F, bytes_accessed=11 * 2**20, transcendentals=0
        ),
    )(sources, targets, count, values, *panels)


def dense_kernel(
    aggregated, cotangent, low_weight, bias, activations, grad_pre, grad_aggregated
):
    w = low_weight[...]
    pre = jnp.dot(aggregated[...], w, preferred_element_type=jnp.float32) + bias[...]
    sigma = jax.nn.sigmoid(pre)
    grad = cotangent[...].astype(jnp.float32) * sigma * (1.0 + pre * (1.0 - sigma))
    low_grad = grad.astype(jnp.bfloat16)
    activations[...] = (pre * sigma).astype(jnp.bfloat16)
    grad_pre[...] = low_grad
    grad_aggregated[...] = lax.dot_general(
        low_grad, w, (((1,), (1,)), ((), ())), preferred_element_type=jnp.float32
    ).astype(jnp.bfloat16)


def dense_call(aggregated, cotangent, low_weight, bias):
    shape = jax.ShapeDtypeStruct(aggregated.shape, jnp.bfloat16)
    return pl.pallas_call(
        dense_kernel,
        out_shape=[shape] * 3,
        compiler_params=pltpu.CompilerParams(vmem_limit_bytes=VMEM_BYTES),
    )(aggregated, cotangent, low_weight, bias)


def swap(value, axis, bit):
    size = lax.axis_size(axis)
    return lax.ppermute(value, axis, [(i, i ^ (1 << bit)) for i in range(size)])


def shift(value, axes, by):
    pairs = []
    for core, axis in enumerate(axes):
        for y in range(4):
            for x in range(4):
                to = (y, (x + by) % 4) if axis == "x" else ((y + by) % 4, x)
                pairs.append((core * 16 + y * 4 + x, core * 16 + to[0] * 4 + to[1]))
    return lax.ppermute(value, ("core", "y", "x"), pairs)


def advance(value):
    pairs = []
    for z in range(Z):
        pairs += [(z * 2, (z + 1) % Z * 2), (z * 2 + 1, (z - 1) % Z * 2 + 1)]
    return lax.ppermute(value, ("z", "core"), pairs)


def wide(value):
    return value.astype(jnp.float32)


def low(value):
    return value.astype(jnp.bfloat16)


def join(*values):
    return jnp.concatenate(values, axis=0)


def gather_z(features):
    own = features.reshape(2, TILE, F)
    other = swap(own, "core", 0)
    one = advance(join(own, other))
    two = advance(one)
    near = swap(join(one, two), "core", 0)
    three = advance(two)
    four = advance(three[:2])
    return [own, other, one, two, three, four, near, swap(join(three, four), "core", 0)]


def scatter_ring(far_up, far_down, up, down, own, axes):
    from_below = shift(far_up, axes, 1)
    from_above = shift(far_down, axes, -1)
    split = far_up.shape[0]
    up_sum = join(low(wide(up[:split]) + wide(from_below)), up[split:])
    down_sum = join(down[:split], low(wide(down[split:]) + wide(from_above)))
    below = shift(up_sum, axes, 1)
    above = shift(down_sum, axes, -1)
    return wide(own) + wide(below) + wide(above)


def scatter_xy(pieces):
    sums = low(scatter_ring(*pieces, ("x", "y")))
    return scatter_ring(sums[4:5], sums[5:6], sums[2:4], sums[6:8], sums[0:2], ("y", "x"))


class GradSum:
    def __init__(self, local):
        self.total = local
        self.steps = []
        for axis, bit in [("core", 0), ("z", 0), ("z", 1), ("z", 2)]:
            self.steps.append((self.halve, axis, bit))
        for axis, bit in [("x", 0), ("x", 1), ("y", 0), ("y", 1)]:
            self.steps.append((self.double, axis, bit))
        for axis, bit in [("z", 2), ("z", 1), ("z", 0), ("core", 0)]:
            self.steps.append((self.regather, axis, bit))

    def halve(self, axis, bit):
        side = lax.axis_index(axis) >> bit & 1
        rows = self.total.shape[0] // 2
        keep = lax.dynamic_slice_in_dim(self.total, side * rows, rows, 0)
        send = lax.dynamic_slice_in_dim(self.total, (1 - side) * rows, rows, 0)
        self.total = keep + swap(send, axis, bit)

    def double(self, axis, bit):
        self.total = self.total + swap(self.total, axis, bit)

    def regather(self, axis, bit):
        self.total = low(self.total)
        side = lax.axis_index(axis) >> bit & 1
        other = swap(self.total, axis, bit)
        self.total = join(
            jnp.where(side == 0, self.total, other), jnp.where(side == 0, other, self.total)
        )

    def step(self):
        method, axis, bit = self.steps.pop(0)
        method(axis, bit)

    def beside(self, message):
        self.total, message = lax.optimization_barrier((self.total, message))
        self.step()
        return message


def gather_ring(own, axes, grad):
    below = shift(own, axes, 1)
    above = shift(own, axes, -1)
    half = own.shape[0] // 2
    below, above = grad.beside((below, above))
    far_first = shift(above[:half], axes, -1)
    far_last = shift(below[half:], axes, 1)
    return [own, below, above, far_first, far_last]


def gather_xy(own, grad):
    grad.step()
    bundle = grad.beside(join(*gather_ring(own, ("x", "y"), grad)))
    return gather_ring(bundle, ("y", "x"), grad)


def scatter_z(own_first, own_last, other_first, other_last, grad):
    first = swap(grad.beside(other_first), "core", 0)
    last = swap(other_last, "core", 0)

    def term(a, b, start, stop):
        return wide(a[start:stop]) + wide(b[start:stop])

    far = advance(grad.beside(low(term(own_first, first, 0, 2))))
    sums = term(own_first, first, 2, 6)
    three = advance(grad.beside(low(join(sums[:2] + wide(far), sums[2:]))))
    two = advance(grad.beside(low(term(own_last, last, 0, 4) + wide(three))))
    one = advance(grad.beside(low(term(own_last, last, 4, 8) + wide(two))))
    one = grad.beside(one)
    return low(term(own_last, last, 8, 10) + wide(one[:2]) + wide(swap(one[2:], "core", 0)))


def per_device(
    features,
    tile_values,
    tile_row,
    tile_col,
    tile_count,
    weight,
    bias,
    second_weight,
    second_bias,
    cotangent,
):
    values = tile_values[0, 0]
    rows_local = tile_row[0, 0]
    cols_local = tile_col[0, 0]
    count = tile_count[0]
    low_weight = weight.astype(jnp.bfloat16)

    partials = product_call(
        False,
        gather_z_place(cols_local),
        scatter_xy_place(rows_local),
        count,
        values,
        gather_z(features),
        [4, 4, 8, 8, 8],
    )
    aggregated = low(scatter_xy(partials)).reshape(-1, F)
    activations, grad_pre, grad_aggregated = dense_call(
        aggregated, cotangent, low_weight, bias.reshape(1, F)
    )

    with_ones = jnp.concatenate(
        [aggregated, jnp.ones((aggregated.shape[0], TILE), jnp.bfloat16)], axis=1
    )
    local_grad = lax.dot_general(
        with_ones, grad_pre, (((0,), (0,)), ((), ())), preferred_element_type=jnp.float32
    )
    grad = GradSum(local_grad)
    grad_panels = gather_xy(grad_aggregated.reshape(-1, TILE, F), grad)
    grad.step()
    grad.step()

    grad_partials = product_call(
        True,
        gather_xy_place(rows_local),
        scatter_z_place(cols_local),
        count,
        values,
        grad_panels,
        [6, 10, 6, 10],
    )
    grad_features = scatter_z(*grad_partials, grad)
    total_grad = wide(grad.total)
    new_weight = refresh(weight, total_grad[:F], second_weight)
    new_bias = refresh(bias, total_grad[F], second_bias)
    return (activations, grad_features.reshape(-1, F), new_weight, new_bias)


def solution(mesh):
    fine = Mesh(mesh.devices.reshape(Z, 2, 4, 4), ("z", "core", "y", "x"))
    row = ("z", "core")
    col = ("y", "x")
    placed = (
        P(col + row, None),
        P(row, col, None, None, None),
        P(row, col, None),
        P(row, col, None),
        P(row, col),
        P(),
        P(),
        P(),
        P(),
        P(row + col, None),
    )
    return jax.shard_map(
        per_device,
        mesh=fine,
        in_specs=placed,
        out_specs=(P(row + col, None), P(col + row, None), P(), P()),
        check_vma=False,
    )
```

```python
import functools

import jax
import jax.numpy as jnp
from jax import lax
from jax.experimental import pallas as pl
from jax.experimental.pallas import tpu as pltpu
from jax.sharding import Mesh, PartitionSpec as P

learn_rate = 0.1
TILE = 128
F = 512
BLOCK_TILES = 32
UNROLL = 4
Z = 8
VMEM_BYTES = 48 * 1024 * 1024


def refresh(param, grad, second):
    moment = 0.9 * second + 0.1 * grad * grad
    return param - learn_rate * grad / (jnp.sqrt(moment) + 1e-06)


def select(index, table):
    return jnp.take(jnp.array(table, jnp.int32), index)


def pick(index, other, same_table, other_table):
    return jnp.where(other == 0, select(index, same_table), select(index, other_table))


def row_tile_parts(t):
    dy = (t // 8 - lax.axis_index("y")) % 4
    dx = (t // 2 % 4 - lax.axis_index("x")) % 4
    x_first = lax.axis_index("core") == 0
    return jnp.where(x_first, dx, dy), jnp.where(x_first, dy, dx), t % 2


def scatter_xy_place(t):
    first, second, half = row_tile_parts(t)
    return select(first, [3, 1, 0, 2]) * 8 + second * 2 + half


def gather_xy_place(t):
    first, second, half = row_tile_parts(t)
    order = [0, 2, 3, 1]
    return select(second, order) * 8 + select(first, order) * 2 + half


def col_tile_parts(t):
    dz = (t // 4 - lax.axis_index("z")) % Z
    core = lax.axis_index("core")
    return dz, core, (t // 2 % 2 != core).astype(jnp.int32), t % 2


def gather_z_place(t):
    dz, core, other, half = col_tile_parts(t)
    behind = jnp.where(core == 0, (Z - dz) % Z, dz)
    return pick(behind, other, [0, 4, 8, 12, 16, 28, 24, 20], [2, 6, 10, 14, 30, 26, 22, 18]) + half


def scatter_z_place(t):
    dz, core, other, half = col_tile_parts(t)
    ahead = jnp.where(core == 0, dz, (Z - dz) % Z)
    return pick(ahead, other, [14, 10, 6, 2, 0, 20, 24, 28], [30, 12, 8, 4, 16, 18, 22, 26]) + half


def slot_loop(count, sources, targets, values, panel, acc, flip):
    contract = ((0,), (0,)) if flip else ((1,), (0,))

    def step(group, carry):
        for part in range(UNROLL):
            k = group * UNROLL + part
            source = sources[k]
            target = jnp.where(k < count, targets[k], BLOCK_TILES)
            for column in range(0, F, 256):
                columns = slice(column, column + 256)
                acc[target, :, columns] += lax.dot_general(
                    values[k],
                    panel[source, :, columns],
                    (contract, ((), ())),
                    preferred_element_type=jnp.float32,
                )
        return carry

    lax.fori_loop(0, (count + UNROLL - 1) // UNROLL, step, 0)


def product_kernel(flip, n_panels, sources, targets, count, values_hbm, *refs):
    panels, refs = refs[:n_panels], refs[n_panels:]
    outs, (values, panel, acc, sems) = refs[:-4], refs[-4:]
    copies = [pltpu.make_async_copy(values_hbm, values, sems.at[0])]
    start = 0
    for i, piece in enumerate(panels):
        tiles = piece.shape[0]
        copies.append(pltpu.make_async_copy(piece, panel.at[pl.ds(start, tiles)], sems.at[i + 1]))
        start += tiles
    for copy in copies:
        copy.start()
    acc[...] = jnp.zeros_like(acc)
    for copy in copies:
        copy.wait()
    slot_loop(count[0], sources, targets, values, panel, acc, flip)
    start = 0
    for out in outs:
        for t in range(out.shape[0]):
            out[t] = acc[start + t].astype(jnp.bfloat16)
        start += out.shape[0]


def product_call(flip, sources, targets, count, values, panels, out_tiles):
    hbm = pl.BlockSpec(memory_space=pl.ANY)
    smem = pl.BlockSpec(memory_space=pltpu.SMEM)
    vmem = pl.BlockSpec(memory_space=pltpu.VMEM)
    slots = values.shape[0]
    return pl.pallas_call(
        functools.partial(product_kernel, flip, len(panels)),
        out_shape=[jax.ShapeDtypeStruct((n, TILE, F), jnp.bfloat16) for n in out_tiles],
        in_specs=[smem] * 3 + [hbm] * (1 + len(panels)),
        out_specs=[vmem] * len(out_tiles),
        scratch_shapes=[
            pltpu.VMEM((slots, TILE, TILE), jnp.bfloat16),
            pltpu.VMEM((BLOCK_TILES, TILE, F), jnp.bfloat16),
            pltpu.VMEM((BLOCK_TILES + 1, TILE, F), jnp.float32),
            pltpu.SemaphoreType.DMA((1 + len(panels),)),
        ],
        compiler_params=pltpu.CompilerParams(vmem_limit_bytes=VMEM_BYTES),
        cost_estimate=pl.CostEstimate(
            flops=8 * slots * TILE * TILE * F, bytes_accessed=32 * 2**20, transcendentals=0
        ),
    )(sources, targets, count, values, *panels)


def dense_kernel(
    aggregated, cotangent, low_weight, bias, activations, grad_pre, grad_aggregated
):
    w = low_weight[...]
    pre = jnp.dot(aggregated[...], w, preferred_element_type=jnp.float32) + bias[...]
    sigma = jax.nn.sigmoid(pre)
    grad = cotangent[...].astype(jnp.float32) * sigma * (1.0 + pre * (1.0 - sigma))
    low_grad = grad.astype(jnp.bfloat16)
    activations[...] = (pre * sigma).astype(jnp.bfloat16)
    grad_pre[...] = low_grad
    grad_aggregated[...] = lax.dot_general(
        low_grad, w, (((1,), (1,)), ((), ())), preferred_element_type=jnp.float32
    ).astype(jnp.bfloat16)


def dense_call(aggregated, cotangent, low_weight, bias):
    shape = jax.ShapeDtypeStruct(aggregated.shape, jnp.bfloat16)
    return pl.pallas_call(
        dense_kernel,
        out_shape=[shape] * 3,
        compiler_params=pltpu.CompilerParams(vmem_limit_bytes=VMEM_BYTES),
    )(aggregated, cotangent, low_weight, bias)


def swap(value, axis, bit):
    size = lax.axis_size(axis)
    return lax.ppermute(value, axis, [(i, i ^ (1 << bit)) for i in range(size)])


def shift(value, axes, by):
    pairs = []
    for core, axis in enumerate(axes):
        for y in range(4):
            for x in range(4):
                to = (y, (x + by) % 4) if axis == "x" else ((y + by) % 4, x)
                pairs.append((core * 16 + y * 4 + x, core * 16 + to[0] * 4 + to[1]))
    return lax.ppermute(value, ("core", "y", "x"), pairs)


def advance(value):
    pairs = []
    for z in range(Z):
        pairs += [(z * 2, (z + 1) % Z * 2), (z * 2 + 1, (z - 1) % Z * 2 + 1)]
    return lax.ppermute(value, ("z", "core"), pairs)


def wide(value):
    return value.astype(jnp.float32)


def low(value):
    return value.astype(jnp.bfloat16)


def join(*values):
    return jnp.concatenate(values, axis=0)


def gather_z(features):
    own = features.reshape(2, TILE, F)
    a1 = advance(own)
    other = swap(own, "core", 0)
    b1 = advance(other)
    a2 = advance(a1)
    b2 = advance(b1)
    a3 = advance(a2)
    b3 = advance(b2)
    near, a4 = lax.optimization_barrier((join(a1, b1, a2, b2), advance(a3)))
    pieces = [own, other, a1, b1, a2, b2, a3, b3, a4]
    return pieces + [swap(near, "core", 0), swap(join(a3, b3, a4), "core", 0)]


def scatter_xy(far_up, far_down, up_a, up_b, down_a, down_b, own):
    axes = ("x", "y")
    from_below = shift(far_up, axes, 1)
    from_above = shift(far_down, axes, -1)
    below_b = shift(up_b, axes, 1)
    above_a = shift(down_a, axes, -1)
    below_a = shift(low(wide(up_a) + wide(from_below)), axes, 1)
    above_b = shift(low(wide(down_b) + wide(from_above)), axes, -1)
    sum_a = low(wide(own[:4]) + wide(below_a) + wide(above_a))
    sum_b = low(wide(own[4:]) + wide(below_b) + wide(above_b))
    axes = ("y", "x")
    own, up, far, down = sum_a[:2], sum_a[2:], sum_b[:2], sum_b[2:]
    from_below = shift(far[:1], axes, 1)
    from_above = shift(far[1:], axes, -1)
    below = shift(join(low(wide(up[:1]) + wide(from_below)), up[1:]), axes, 1)
    above = shift(join(down[:1], low(wide(down[1:]) + wide(from_above))), axes, -1)
    return wide(own) + wide(below) + wide(above)


def gather_xy(own, grad):
    axes = ("x", "y")
    below, above = shift(own, axes, 1), shift(own, axes, -1)
    grad.halve("core", 0)
    below, above = grad.beside((below, above))
    far_first = shift(above[:1], axes, -1)
    far_last = shift(below[1:], axes, 1)
    grad.halve("z", 0)
    axes = ("y", "x")
    first = join(own, below)
    above_first, below_first = shift(first, axes, -1), shift(first, axes, 1)
    last = grad.beside(join(above, far_first, far_last))
    below_last, above_last = shift(last, axes, 1), shift(last, axes, -1)
    grad.halve("z", 1)
    above_first, below_last = grad.beside((above_first, below_last))
    far = [shift(above_first, axes, -1), shift(below_last, axes, 1)]
    grad.halve("z", 2)
    grad.double("x", 0)
    panels = grad.beside([first, last, below_first, below_last, above_first, above_last] + far)
    grad.double("x", 1)
    return panels


class GradSum:
    def __init__(self, local):
        self.total = local

    def beside(self, message):
        self.total, message = lax.optimization_barrier((self.total, message))
        return message

    def halve(self, axis, bit):
        side = lax.axis_index(axis) >> bit & 1
        rows = self.total.shape[0] // 2
        keep = lax.dynamic_slice_in_dim(self.total, side * rows, rows, 0)
        send = lax.dynamic_slice_in_dim(self.total, (1 - side) * rows, rows, 0)
        self.total = keep + wide(swap(low(send), axis, bit))

    def double(self, axis, bit):
        self.total = self.total + swap(self.total, axis, bit)

    def regather(self, axis, bit):
        self.total = low(self.total)
        side = lax.axis_index(axis) >> bit & 1
        other = swap(self.total, axis, bit)
        self.total = join(
            jnp.where(side == 0, self.total, other), jnp.where(side == 0, other, self.total)
        )


def scatter_z(own_first, own_last, other_first, other_last, grad):
    first = swap(grad.beside(other_first), "core", 0)
    last = swap(other_last, "core", 0)
    grad.double("y", 0)

    def term(a, b, start):
        return wide(a[start : start + 2]) + wide(b[start : start + 2])

    a = advance(grad.beside(low(term(own_first, first, 0))))
    grad.double("y", 1)
    b = advance(low(term(own_first, first, 4)))
    a = advance(grad.beside(low(term(own_first, first, 2) + wide(a))))
    grad.regather("z", 2)
    b = advance(low(term(own_last, last, 2) + wide(b)))
    a = advance(grad.beside(low(term(own_last, last, 0) + wide(a))))
    grad.regather("z", 1)
    b = advance(low(term(own_last, last, 6) + wide(b)))
    a = advance(grad.beside(low(term(own_last, last, 4) + wide(a))))
    grad.regather("z", 0)
    b = swap(grad.beside(b), "core", 0)
    grad.regather("core", 0)
    return low(term(own_last, last, 8) + wide(a) + wide(b))


def per_device(
    features,
    tile_values,
    tile_row,
    tile_col,
    tile_count,
    weight,
    bias,
    second_weight,
    second_bias,
    cotangent,
):
    values = tile_values[0, 0]
    rows_local = tile_row[0, 0]
    cols_local = tile_col[0, 0]
    count = tile_count[0]
    low_weight = weight.astype(jnp.bfloat16)

    partials = product_call(
        False,
        gather_z_place(cols_local),
        scatter_xy_place(rows_local),
        count,
        values,
        gather_z(features),
        [4, 4, 4, 4, 4, 4, 8],
    )
    aggregated = low(scatter_xy(*partials)).reshape(-1, F)
    activations, grad_pre, grad_aggregated = dense_call(
        aggregated, cotangent, low_weight, bias.reshape(1, F)
    )

    with_ones = jnp.concatenate(
        [aggregated, jnp.ones((aggregated.shape[0], TILE), jnp.bfloat16)], axis=1
    )
    local_grad = lax.dot_general(
        with_ones, grad_pre, (((0,), (0,)), ((), ())), preferred_element_type=jnp.float32
    )
    grad = GradSum(local_grad)
    grad_panels = gather_xy(grad_aggregated.reshape(-1, TILE, F), grad)

    grad_partials = product_call(
        True,
        gather_xy_place(rows_local),
        scatter_z_place(cols_local),
        count,
        values,
        grad_panels,
        [6, 10, 6, 10],
    )
    grad_features = scatter_z(*grad_partials, grad)
    total_grad = wide(grad.total)
    new_weight = refresh(weight, total_grad[:F], second_weight)
    new_bias = refresh(bias, total_grad[F], second_bias)
    return (activations, grad_features.reshape(-1, F), new_weight, new_bias)


def solution(mesh):
    fine = Mesh(mesh.devices.reshape(Z, 2, 4, 4), ("z", "core", "y", "x"))
    row = ("z", "core")
    col = ("y", "x")
    placed = (
        P(col + row, None),
        P(row, col, None, None, None),
        P(row, col, None),
        P(row, col, None),
        P(row, col),
        P(),
        P(),
        P(),
        P(),
        P(row + col, None),
    )
    return jax.shard_map(
        per_device,
        mesh=fine,
        in_specs=placed,
        out_specs=(P(row + col, None), P(col + row, None), P(), P()),
        check_vma=False,
    )
```

```python
import functools

import jax
import jax.numpy as jnp
from jax import lax
from jax.experimental import pallas as pl
from jax.experimental.pallas import tpu as pltpu
from jax.sharding import Mesh, PartitionSpec as P

learn_rate = 0.1
TILE = 128
F = 512
BLOCK_TILES = 32
UNROLL = 4
Z = 8
VMEM_BYTES = 28 * 1024 * 1024


def refresh(param, grad, second):
    moment = 0.9 * second + 0.1 * grad * grad
    return param - learn_rate * grad / (jnp.sqrt(moment) + 1e-06)


def select(index, table):
    return jnp.take(jnp.array(table, jnp.int32), index)


def pick(index, other, same_table, other_table):
    return jnp.where(other == 0, select(index, same_table), select(index, other_table))


def row_tile_parts(t):
    dy = (t // 8 - lax.axis_index("y")) % 4
    dx = (t // 2 % 4 - lax.axis_index("x")) % 4
    x_first = lax.axis_index("core") == 0
    return jnp.where(x_first, dx, dy), jnp.where(x_first, dy, dx), t % 2


def scatter_xy_place(t):
    first, second, half = row_tile_parts(t)
    return select(first, [3, 1, 0, 2]) * 8 + second * 2 + half


def gather_xy_place(t):
    first, second, half = row_tile_parts(t)
    order = [0, 2, 3, 1]
    return select(second, order) * 8 + select(first, order) * 2 + half


def col_tile_parts(t):
    dz = (t // 4 - lax.axis_index("z")) % Z
    core = lax.axis_index("core")
    return dz, core, (t // 2 % 2 != core).astype(jnp.int32), t % 2


def gather_z_place(t):
    dz, core, other, half = col_tile_parts(t)
    behind = jnp.where(core == 0, (Z - dz) % Z, dz)
    return pick(behind, other, [0, 4, 8, 12, 16, 28, 24, 20], [2, 6, 10, 14, 30, 26, 22, 18]) + half


def scatter_z_place(t):
    dz, core, other, half = col_tile_parts(t)
    ahead = jnp.where(core == 0, dz, (Z - dz) % Z)
    return pick(ahead, other, [30, 28, 24, 10, 8, 4, 6, 18], [22, 26, 14, 12, 0, 2, 16, 20]) + half


def slot_order(first):
    index = jnp.arange(first.shape[0], dtype=jnp.int32)
    later = (~first).astype(jnp.int32)
    key = later * first.shape[0] + index
    rank = jnp.sum((key[None, :] < key[:, None]).astype(jnp.int32), axis=1)
    return jnp.sum(jnp.where(rank[None, :] == index[:, None], index[None, :], 0), axis=1)


def slot_loop(start, stop, order, sources, targets, base, values, panel, acc, flip):
    contract = ((0,), (0,)) if flip else ((1,), (0,))
    spare = acc.shape[0] - 1
    last = values.shape[0] - 1

    def step(group, carry):
        for part in range(UNROLL):
            i = start + group * UNROLL + part
            k = order[jnp.minimum(i, last)]
            source = sources[k]
            target = jnp.where(i < stop, targets[k] - base, spare)
            for column in range(0, F, 256):
                columns = slice(column, column + 256)
                acc[target, :, columns] += lax.dot_general(
                    values[k],
                    panel[source, :, columns],
                    (contract, ((), ())),
                    preferred_element_type=jnp.float32,
                )
        return carry

    lax.fori_loop(0, (stop - start + UNROLL - 1) // UNROLL, step, 0)


def write_out(acc, outs):
    start = 0
    for out in outs:
        for t in range(out.shape[0]):
            out[t] = acc[start + t].astype(out.dtype)
        start += out.shape[0]


def first_kernel(flip, n_panels, order, sources, targets, counts, values, *refs):
    panels, refs = refs[:n_panels], refs[n_panels:]
    outs, panel, acc, sems = refs[:-3], refs[-3], refs[-2], refs[-1]
    copies = []
    start = 0
    for i, piece in enumerate(panels):
        tiles = piece.shape[0]
        copies.append(pltpu.make_async_copy(piece, panel.at[pl.ds(start, tiles)], sems.at[i]))
        start += tiles
    for copy in copies:
        copy.start()
    acc[...] = jnp.zeros_like(acc)
    for copy in copies:
        copy.wait()
    slot_loop(0, counts[0], order, sources, targets, 0, values, panel, acc, flip)
    write_out(acc, outs)


def second_kernel(flip, base, order, sources, targets, counts, values, panel, *refs):
    outs, acc = refs[:-1], refs[-1]
    acc[...] = jnp.zeros_like(acc)
    slot_loop(counts[0], counts[1], order, sources, targets, base, values, panel, acc, flip)
    write_out(acc, outs)


def product_calls(flip, sources, targets, count, values, panels, first_tiles, second_tiles):
    hbm = pl.BlockSpec(memory_space=pl.ANY)
    smem = pl.BlockSpec(memory_space=pltpu.SMEM)
    vmem = pl.BlockSpec(memory_space=pltpu.VMEM)
    slots = values.shape[0]
    base = sum(first_tiles)
    is_first = (targets < base) & (jnp.arange(slots) < count)
    scalars = (
        slot_order(is_first),
        sources,
        targets,
        jnp.stack([jnp.sum(is_first, dtype=jnp.int32), count]),
    )
    params = pltpu.CompilerParams(vmem_limit_bytes=VMEM_BYTES)
    cost = pl.CostEstimate(
        flops=4 * slots * TILE * TILE * F, bytes_accessed=16 * 2**20, transcendentals=0
    )

    def tiles_of(counts, last=jnp.bfloat16):
        dtypes = [jnp.bfloat16] * (len(counts) - 1) + [last]
        return [jax.ShapeDtypeStruct((n, TILE, F), d) for n, d in zip(counts, dtypes)]

    *first, panel = pl.pallas_call(
        functools.partial(first_kernel, flip, len(panels)),
        out_shape=tiles_of(first_tiles + [BLOCK_TILES]),
        in_specs=[smem] * 4 + [vmem] + [hbm] * len(panels),
        out_specs=[vmem] * (len(first_tiles) + 1),
        scratch_shapes=[
            pltpu.VMEM((base + 1, TILE, F), jnp.float32),
            pltpu.SemaphoreType.DMA((len(panels),)),
        ],
        compiler_params=params,
        cost_estimate=cost,
    )(*scalars, values, *panels)

    def finish(panel):
        return pl.pallas_call(
            functools.partial(second_kernel, flip, base),
            out_shape=tiles_of(second_tiles, jnp.bfloat16 if flip else jnp.float32),
            in_specs=[smem] * 4 + [vmem] * 2,
            out_specs=[vmem] * len(second_tiles),
            scratch_shapes=[pltpu.VMEM((BLOCK_TILES - base + 1, TILE, F), jnp.float32)],
            compiler_params=params,
            cost_estimate=cost,
        )(*scalars, values, panel)

    return first, panel, finish


def dense_kernel(
    aggregated, cotangent, low_weight, bias, activations, grad_pre, grad_aggregated
):
    w = low_weight[...]
    pre = jnp.dot(aggregated[...], w, preferred_element_type=jnp.float32) + bias[...]
    sigma = jax.nn.sigmoid(pre)
    grad = cotangent[...].astype(jnp.float32) * sigma * (1.0 + pre * (1.0 - sigma))
    low_grad = grad.astype(jnp.bfloat16)
    activations[...] = (pre * sigma).astype(jnp.bfloat16)
    grad_pre[...] = low_grad
    grad_aggregated[...] = lax.dot_general(
        low_grad, w, (((1,), (1,)), ((), ())), preferred_element_type=jnp.float32
    ).astype(jnp.bfloat16)


def dense_call(aggregated, cotangent, low_weight, bias):
    shape = jax.ShapeDtypeStruct(aggregated.shape, jnp.bfloat16)
    return pl.pallas_call(
        dense_kernel,
        out_shape=[shape] * 3,
        compiler_params=pltpu.CompilerParams(vmem_limit_bytes=VMEM_BYTES),
    )(aggregated, cotangent, low_weight, bias)


def swap(value, axis, bit):
    size = lax.axis_size(axis)
    return lax.ppermute(value, axis, [(i, i ^ (1 << bit)) for i in range(size)])


def shift(value, axes, by):
    pairs = []
    for core, axis in enumerate(axes):
        for y in range(4):
            for x in range(4):
                to = (y, (x + by) % 4) if axis == "x" else ((y + by) % 4, x)
                pairs.append((core * 16 + y * 4 + x, core * 16 + to[0] * 4 + to[1]))
    return lax.ppermute(value, ("core", "y", "x"), pairs)


def advance(value):
    pairs = []
    for z in range(Z):
        pairs += [(z * 2, (z + 1) % Z * 2), (z * 2 + 1, (z - 1) % Z * 2 + 1)]
    return lax.ppermute(value, ("z", "core"), pairs)


def wide(value):
    return value.astype(jnp.float32)


def low(value):
    return value.astype(jnp.bfloat16)


def join(*values):
    return jnp.concatenate(values, axis=0)


def gather_z(features):
    own = features.reshape(2, TILE, F)
    a1 = advance(own)
    other = swap(own, "core", 0)
    b1 = advance(other)
    a2 = advance(a1)
    b2 = advance(b1)
    a3 = advance(a2)
    b3 = advance(b2)
    near, a4 = lax.optimization_barrier((join(a1, b1, a2, b2), advance(a3)))
    pieces = [own, other, a1, b1, a2, b2, a3, b3, a4]
    return pieces + [swap(near, "core", 0), swap(join(a3, b3, a4), "core", 0)]


def scatter_xy(far_up, far_down, up_a, up_b, down_a, down_b, own):
    axes = ("x", "y")
    from_below = shift(far_up, axes, 1)
    from_above = shift(far_down, axes, -1)
    below_b = shift(up_b, axes, 1)
    above_a = shift(down_a, axes, -1)
    below_a = shift(low(wide(up_a) + wide(from_below)), axes, 1)
    above_b = shift(low(wide(down_b) + wide(from_above)), axes, -1)
    sum_a = own[:4] + wide(below_a) + wide(above_a)
    sum_b = low(own[4:] + wide(below_b) + wide(above_b))
    axes = ("y", "x")
    own, up, far, down = sum_a[:2], low(sum_a[2:]), sum_b[:2], sum_b[2:]
    from_below = shift(far[:1], axes, 1)
    from_above = shift(far[1:], axes, -1)
    below = shift(join(low(wide(up[:1]) + wide(from_below)), up[1:]), axes, 1)
    above = shift(join(down[:1], low(wide(down[1:]) + wide(from_above))), axes, -1)
    return own + wide(below) + wide(above)


def gather_xy(own, grad):
    axes = ("x", "y")
    below, above = shift(own, axes, 1), shift(own, axes, -1)
    grad.halve("core", 0)
    below, above = grad.beside((below, above))
    far_first = shift(above[:1], axes, -1)
    far_last = shift(below[1:], axes, 1)
    grad.halve("z", 0)
    axes = ("y", "x")
    first = join(own, below)
    above_first, below_first = shift(first, axes, -1), shift(first, axes, 1)
    last = grad.beside(join(above, far_first, far_last))
    below_last, above_last = shift(last, axes, 1), shift(last, axes, -1)
    grad.halve("z", 1)
    above_first, below_last = grad.beside((above_first, below_last))
    far = [shift(above_first, axes, -1), shift(below_last, axes, 1)]
    grad.halve("z", 2)
    grad.double("x", 0)
    panels = grad.beside([first, last, below_first, below_last, above_first, above_last] + far)
    grad.double("x", 1)
    return panels


class GradSum:
    def __init__(self, local):
        self.total = local

    def beside(self, message):
        self.total, message = lax.optimization_barrier((self.total, message))
        return message

    def halve(self, axis, bit):
        side = lax.axis_index(axis) >> bit & 1
        rows = self.total.shape[0] // 2
        keep = lax.dynamic_slice_in_dim(self.total, side * rows, rows, 0)
        send = lax.dynamic_slice_in_dim(self.total, (1 - side) * rows, rows, 0)
        message = send if axis == "core" else low(send)
        self.total = keep + wide(swap(message, axis, bit))

    def double(self, axis, bit):
        self.total = self.total + swap(self.total, axis, bit)

    def regather(self, axis, bit):
        self.total = low(self.total)
        side = lax.axis_index(axis) >> bit & 1
        other = swap(self.total, axis, bit)
        self.total = join(
            jnp.where(side == 0, self.total, other), jnp.where(side == 0, other, self.total)
        )


def scatter_z(other_first, own_first, panel, finish, grad):
    first = swap(grad.beside(other_first), "core", 0)
    grad.double("y", 0)

    def term(a, b, start):
        return wide(a[start : start + 2]) + wide(b[start : start + 2])

    a, b, panel = grad.beside(
        (low(term(own_first, first, 0)), low(term(own_first, first, 4)), panel)
    )
    a, b = advance(a), advance(b)
    grad.double("y", 1)
    other_next, other_last, own_next, own_last = finish(panel)
    near = swap(other_next, "core", 0)
    last = swap(other_last, "core", 0)
    a = advance(grad.beside(low(term(own_first, first, 2) + wide(a))))
    grad.regather("z", 2)
    b = advance(low(term(own_first, first, 6) + wide(b)))
    a = advance(grad.beside(low(term(own_next, near, 0) + wide(a))))
    grad.regather("z", 1)
    b = advance(low(term(own_next, near, 2) + wide(b)))
    a = advance(grad.beside(low(term(own_last, last, 0) + wide(a))))
    grad.regather("z", 0)
    b = swap(grad.beside(b), "core", 0)
    grad.regather("core", 0)
    return low(term(own_last, last, 2) + wide(a) + wide(b))


def per_device(
    features,
    tile_values,
    tile_row,
    tile_col,
    tile_count,
    weight,
    bias,
    second_weight,
    second_bias,
    cotangent,
):
    values = tile_values[0, 0]
    rows_local = tile_row[0, 0]
    cols_local = tile_col[0, 0]
    count = tile_count[0, 0]
    low_weight = weight.astype(jnp.bfloat16)

    first, panel, finish = product_calls(
        False,
        gather_z_place(cols_local),
        scatter_xy_place(rows_local),
        count,
        values,
        gather_z(features),
        [4, 4],
        [4, 4, 4, 4, 8],
    )
    aggregated = low(scatter_xy(*first, *finish(panel))).reshape(-1, F)
    activations, grad_pre, grad_aggregated = dense_call(
        aggregated, cotangent, low_weight, bias.reshape(1, F)
    )

    with_ones = jnp.concatenate(
        [aggregated, jnp.ones((aggregated.shape[0], TILE), jnp.bfloat16)], axis=1
    )
    local_grad = lax.dot_general(
        with_ones, grad_pre, (((0,), (0,)), ((), ())), preferred_element_type=jnp.float32
    )
    grad = GradSum(local_grad)
    grad_panels = gather_xy(grad_aggregated.reshape(-1, TILE, F), grad)

    first, panel, finish = product_calls(
        True,
        gather_xy_place(rows_local),
        scatter_z_place(cols_local),
        count,
        values,
        grad_panels,
        [8, 8],
        [4, 4, 4, 4],
    )
    grad_features = scatter_z(*first, panel, finish, grad)
    total_grad = wide(grad.total)
    new_weight = refresh(weight, total_grad[:F], second_weight)
    new_bias = refresh(bias, total_grad[F], second_bias)
    return (activations, grad_features.reshape(-1, F), new_weight, new_bias)


def solution(mesh):
    fine = Mesh(mesh.devices.reshape(Z, 2, 4, 4), ("z", "core", "y", "x"))
    row = ("z", "core")
    col = ("y", "x")
    placed = (
        P(col + row, None),
        P(row, col, None, None, None),
        P(row, col, None),
        P(row, col, None),
        P(row, col),
        P(),
        P(),
        P(),
        P(),
        P(row + col, None),
    )
    return jax.shard_map(
        per_device,
        mesh=fine,
        in_specs=placed,
        out_specs=(P(row + col, None), P(col + row, None), P(), P()),
        check_vma=False,
    )
```

```python
import functools

import jax
import jax.numpy as jnp
from jax import lax
from jax.experimental import pallas as pl
from jax.experimental.pallas import tpu as pltpu
from jax.sharding import Mesh, PartitionSpec as P

learn_rate = 0.1
TILE = 128
F = 512
BLOCK_TILES = 32
UNROLL = 4
Z = 8
VMEM_BYTES = 28 * 1024 * 1024


def refresh(param, grad, second):
    moment = 0.9 * second + 0.1 * grad * grad
    return param - learn_rate * grad / (jnp.sqrt(moment) + 1e-06)


def select(index, table):
    return jnp.take(jnp.array(table, jnp.int32), index)


def pick(index, other, same_table, other_table):
    return jnp.where(other == 0, select(index, same_table), select(index, other_table))


def row_tile_parts(t):
    dy = (t // 8 - lax.axis_index("y")) % 4
    dx = (t // 2 % 4 - lax.axis_index("x")) % 4
    x_first = lax.axis_index("core") == 0
    return jnp.where(x_first, dx, dy), jnp.where(x_first, dy, dx), t % 2


def scatter_xy_place(t):
    first, second, half = row_tile_parts(t)
    return select(first, [3, 1, 0, 2]) * 8 + second * 2 + half


def gather_xy_place(t):
    first, second, half = row_tile_parts(t)
    order = [0, 2, 3, 1]
    return select(second, order) * 8 + select(first, order) * 2 + half


def col_tile_parts(t):
    core = t // 2 % 2
    dz = (t // 4 - lax.axis_index("z")) % Z
    ahead = jnp.where(core == 0, dz, (Z - dz) % Z)
    return ahead, (core != lax.axis_index("core")).astype(jnp.int32), t % 2


def gather_z_place(t):
    core = lax.axis_index("core")
    dz = (t // 4 - lax.axis_index("z")) % Z
    other, half = (t // 2 % 2 != core).astype(jnp.int32), t % 2
    behind = jnp.where(core == 0, (Z - dz) % Z, dz)
    same = select(behind, [0, 4, 8, 12, 16, 28, 24, 20])
    return jnp.where(other == 0, same, select(behind, [2, 6, 10, 14, 30, 26, 22, 18])) + half


def scatter_z_place(t):
    ahead, other, half = col_tile_parts(t)
    same = select(ahead, [30, 28, 24, 10, 8, 12, 14, 26])
    return jnp.where(other == 0, same, same - 8) + half


def slot_order(first):
    index = jnp.arange(first.shape[0], dtype=jnp.int32)
    later = (~first).astype(jnp.int32)
    key = later * first.shape[0] + index
    rank = jnp.sum((key[None, :] < key[:, None]).astype(jnp.int32), axis=1)
    return jnp.sum(jnp.where(rank[None, :] == index[:, None], index[None, :], 0), axis=1)


def slot_loop(start, stop, order, sources, targets, base, values, panel, acc, flip):
    contract = ((0,), (0,)) if flip else ((1,), (0,))
    spare = acc.shape[0] - 1
    last = values.shape[0] - 1

    def step(group, carry):
        for part in range(UNROLL):
            i = start + group * UNROLL + part
            k = order[jnp.minimum(i, last)]
            source = sources[k]
            target = jnp.where(i < stop, targets[k] - base, spare)
            for column in range(0, F, 256):
                columns = slice(column, column + 256)
                acc[target, :, columns] += lax.dot_general(
                    values[k],
                    panel[source, :, columns],
                    (contract, ((), ())),
                    preferred_element_type=jnp.float32,
                )
        return carry

    lax.fori_loop(0, (stop - start + UNROLL - 1) // UNROLL, step, 0)


def write_out(acc, outs):
    start = 0
    for out in outs:
        for t in range(out.shape[0]):
            out[t] = acc[start + t].astype(out.dtype)
        start += out.shape[0]


def first_kernel(flip, n_panels, order, sources, targets, counts, values, *refs):
    panels, refs = refs[:n_panels], refs[n_panels:]
    outs, panel, acc, sems = refs[:-3], refs[-3], refs[-2], refs[-1]
    copies = []
    start = 0
    for i, piece in enumerate(panels):
        tiles = piece.shape[0]
        copies.append(pltpu.make_async_copy(piece, panel.at[pl.ds(start, tiles)], sems.at[i]))
        start += tiles
    for copy in copies:
        copy.start()
    acc[...] = jnp.zeros_like(acc)
    for copy in copies:
        copy.wait()
    slot_loop(0, counts[0], order, sources, targets, 0, values, panel, acc, flip)
    write_out(acc, outs)


def second_kernel(flip, base, order, sources, targets, counts, values, panel, *refs):
    outs, acc = refs[:-1], refs[-1]
    acc[...] = jnp.zeros_like(acc)
    slot_loop(counts[0], counts[1], order, sources, targets, base, values, panel, acc, flip)
    write_out(acc, outs)


def product_calls(flip, sources, targets, count, values, panels, first_tiles, second_tiles):
    hbm = pl.BlockSpec(memory_space=pltpu.HBM if flip else pl.ANY)
    smem = pl.BlockSpec(memory_space=pltpu.SMEM)
    vmem = pl.BlockSpec(memory_space=pltpu.VMEM)
    slots = values.shape[0]
    base = sum(first_tiles)
    is_first = (targets < base) & (jnp.arange(slots) < count)
    scalars = (
        slot_order(is_first),
        sources,
        targets,
        jnp.stack([jnp.sum(is_first, dtype=jnp.int32), count]),
    )
    params = pltpu.CompilerParams(vmem_limit_bytes=VMEM_BYTES)
    cost = pl.CostEstimate(
        flops=4 * slots * TILE * TILE * F, bytes_accessed=16 * 2**20, transcendentals=0
    )

    def tiles_of(counts, last=jnp.bfloat16):
        dtypes = [jnp.bfloat16] * (len(counts) - 1) + [last]
        return [jax.ShapeDtypeStruct((n, TILE, F), d) for n, d in zip(counts, dtypes)]

    *first, panel = pl.pallas_call(
        functools.partial(first_kernel, flip, len(panels)),
        out_shape=tiles_of(first_tiles + [BLOCK_TILES]),
        in_specs=[smem] * 4 + [vmem] + [hbm] * len(panels),
        out_specs=[vmem] * (len(first_tiles) + 1),
        scratch_shapes=[
            pltpu.VMEM((base + 1, TILE, F), jnp.float32),
            pltpu.SemaphoreType.DMA((len(panels),)),
        ],
        compiler_params=params,
        cost_estimate=cost,
    )(*scalars, values, *panels)

    def finish(panel):
        return pl.pallas_call(
            functools.partial(second_kernel, flip, base),
            out_shape=tiles_of(second_tiles, jnp.bfloat16 if flip else jnp.float32),
            in_specs=[smem] * 4 + [vmem] * 2,
            out_specs=[vmem] * len(second_tiles),
            scratch_shapes=[pltpu.VMEM((BLOCK_TILES - base + 1, TILE, F), jnp.float32)],
            compiler_params=params,
            cost_estimate=cost,
        )(*scalars, values, panel)

    return first, panel, finish


def dense_kernel(
    aggregated, cotangent, low_weight, bias, activations, grad_pre, grad_aggregated
):
    w = low_weight[...]
    pre = jnp.dot(aggregated[...], w, preferred_element_type=jnp.float32) + bias[...]
    sigma = jax.nn.sigmoid(pre)
    grad = cotangent[...].astype(jnp.float32) * sigma * (1.0 + pre * (1.0 - sigma))
    low_grad = grad.astype(jnp.bfloat16)
    activations[...] = (pre * sigma).astype(jnp.bfloat16)
    grad_pre[...] = low_grad
    grad_aggregated[...] = lax.dot_general(
        low_grad, w, (((1,), (1,)), ((), ())), preferred_element_type=jnp.float32
    ).astype(jnp.bfloat16)


def dense_call(aggregated, cotangent, low_weight, bias):
    shape = jax.ShapeDtypeStruct(aggregated.shape, jnp.bfloat16)
    return pl.pallas_call(
        dense_kernel,
        out_shape=[shape] * 3,
        compiler_params=pltpu.CompilerParams(vmem_limit_bytes=VMEM_BYTES),
    )(aggregated, cotangent, low_weight, bias)


def swap(value, axis, bit):
    size = lax.axis_size(axis)
    return lax.ppermute(value, axis, [(i, i ^ (1 << bit)) for i in range(size)])


def shift(value, axes, by):
    pairs = []
    for core, axis in enumerate(axes):
        for y in range(4):
            for x in range(4):
                to = (y, (x + by) % 4) if axis == "x" else ((y + by) % 4, x)
                pairs.append((core * 16 + y * 4 + x, core * 16 + to[0] * 4 + to[1]))
    return lax.ppermute(value, ("core", "y", "x"), pairs)


def along_z(value, by):
    pairs = []
    for z in range(Z):
        pairs += [(z * 2, (z + by) % Z * 2), (z * 2 + 1, (z - by) % Z * 2 + 1)]
    return lax.ppermute(value, ("z", "core"), pairs)


def wide(value):
    return value.astype(jnp.float32)


def low(value):
    return value.astype(jnp.bfloat16)


def join(*values):
    return jnp.concatenate(values, axis=0)


def gather_z(features):
    own = features.reshape(2, TILE, F)
    a1 = along_z(own, 1)
    other = swap(own, "core", 0)
    b1 = along_z(other, 1)
    a2 = along_z(a1, 1)
    b2 = along_z(b1, 1)
    a3 = along_z(a2, 1)
    b3 = along_z(b2, 1)
    near, a4 = lax.optimization_barrier((join(a1, b1, a2, b2), along_z(a3, 1)))
    pieces = [own, other, a1, b1, a2, b2, a3, b3, a4]
    return pieces + [swap(near, "core", 0), swap(join(a3, b3, a4), "core", 0)]


def scatter_xy(far_up, far_down, up_a, up_b, down_a, down_b, own):
    axes = ("x", "y")
    from_below = shift(far_up, axes, 1)
    from_above = shift(far_down, axes, -1)
    below_b = shift(up_b, axes, 1)
    above_a = shift(down_a, axes, -1)
    below_a = shift(low(wide(up_a) + wide(from_below)), axes, 1)
    above_b = shift(low(wide(down_b) + wide(from_above)), axes, -1)
    sum_a = own[:4] + wide(below_a) + wide(above_a)
    sum_b = low(own[4:] + wide(below_b) + wide(above_b))
    axes = ("y", "x")
    own, up, far, down = sum_a[:2], low(sum_a[2:]), sum_b[:2], sum_b[2:]
    from_below = shift(far[:1], axes, 1)
    from_above = shift(far[1:], axes, -1)
    below = shift(join(low(wide(up[:1]) + wide(from_below)), up[1:]), axes, 1)
    above = shift(join(down[:1], low(wide(down[1:]) + wide(from_above))), axes, -1)
    return own + wide(below) + wide(above)


def gather_xy(own, grad):
    axes = ("x", "y")
    below, above = shift(own, axes, 1), shift(own, axes, -1)
    grad.next()
    below, above = grad.beside((below, above))
    grad.next()
    far_first = shift(above[:1], axes, -1)
    far_last = shift(below[1:], axes, 1)
    axes = ("y", "x")
    first = join(own, below)
    above_first, below_first = shift(first, axes, -1), shift(first, axes, 1)
    last = join(above, far_first, far_last)
    below_last, above_last = shift(last, axes, 1), shift(last, axes, -1)
    far = [shift(above_first, axes, -1), shift(below_last, axes, 1)]
    panels = [first, last, below_first, below_last, above_first, above_last] + far
    panels = grad.beside(panels)
    grad.next()
    return panels


class GradSum:
    def __init__(self, local):
        self.total = local
        self.steps = [self.halve, self.scatter, self.sum_xy, self.regather_z, self.regather]

    def next(self):
        self.steps.pop(0)()

    def beside(self, message):
        self.total, message = lax.optimization_barrier((self.total, message))
        return message

    def halve(self):
        side = lax.axis_index("core")
        rows = self.total.shape[0] // 2
        keep = lax.dynamic_slice_in_dim(self.total, side * rows, rows, 0)
        send = lax.dynamic_slice_in_dim(self.total, (1 - side) * rows, rows, 0)
        self.total = keep + swap(send, "core", 0)

    def scatter(self):
        terms = lax.all_to_all(low(self.total), "z", split_axis=0, concat_axis=0, tiled=True)
        self.total = jnp.sum(wide(terms).reshape(Z, -1, F), axis=0)

    def to_all(self, block, axes, size):
        blocks = jnp.broadcast_to(block[None], (size,) + block.shape)
        return lax.all_to_all(blocks, axes, split_axis=0, concat_axis=0, tiled=True)

    def sum_xy(self):
        self.total = jnp.sum(self.to_all(self.total, ("y", "x"), 16), axis=0)

    def regather_z(self):
        self.total = self.to_all(low(self.total), "z", Z).reshape(-1, F)

    def regather(self):
        first = lax.axis_index("core") == 0
        other = swap(self.total, "core", 0)
        self.total = join(
            jnp.where(first, self.total, other), jnp.where(first, other, self.total)
        )


def scatter_z(other_first, own_first, panel, finish, grad):
    first = swap(other_first, "core", 0)

    def term(a, b, start):
        return wide(a[start : start + 2]) + wide(b[start : start + 2])

    a, b, panel = lax.optimization_barrier(
        (low(term(own_first, first, 0)), low(term(own_first, first, 4)), panel)
    )
    a, b = along_z(a, 1), along_z(b, -1)
    other_next, other_last, own_next, own_last = finish(panel)
    near = swap(other_next, "core", 0)
    last = swap(other_last, "core", 0)
    a = along_z(grad.beside(low(term(own_first, first, 2) + wide(a))), 1)
    grad.next()
    b = along_z(low(term(own_first, first, 6) + wide(b)), -1)
    a = along_z(low(term(own_next, near, 0) + wide(a)), 1)
    b = along_z(low(term(own_next, near, 2) + wide(b)), -1)
    a = along_z(grad.beside(low(term(own_last, last, 0) + wide(a))), 1)
    grad.next()
    return low(term(own_last, last, 2) + wide(a) + wide(b))


def per_device(
    features,
    tile_values,
    tile_row,
    tile_col,
    tile_count,
    weight,
    bias,
    second_weight,
    second_bias,
    cotangent,
):
    values = tile_values[0, 0]
    rows_local = tile_row[0, 0]
    cols_local = tile_col[0, 0]
    count = tile_count[0, 0]
    low_weight = weight.astype(jnp.bfloat16)

    first, panel, finish = product_calls(
        False,
        gather_z_place(cols_local),
        scatter_xy_place(rows_local),
        count,
        values,
        gather_z(features),
        [4, 4],
        [4, 4, 4, 4, 8],
    )
    aggregated = low(scatter_xy(*first, *finish(panel))).reshape(-1, F)
    activations, grad_pre, grad_aggregated = dense_call(
        aggregated, cotangent, low_weight, bias.reshape(1, F)
    )

    with_ones = jnp.concatenate(
        [aggregated, jnp.ones((aggregated.shape[0], TILE), jnp.bfloat16)], axis=1
    )
    local_grad = lax.dot_general(
        with_ones, grad_pre, (((0,), (0,)), ((), ())), preferred_element_type=jnp.float32
    )
    grad = GradSum(local_grad)
    grad_panels = gather_xy(grad_aggregated.reshape(-1, TILE, F), grad)

    first, panel, finish = product_calls(
        True,
        gather_xy_place(rows_local),
        scatter_z_place(cols_local),
        count,
        values,
        grad_panels,
        [8, 8],
        [4, 4, 4, 4],
    )
    grad_features = scatter_z(*first, panel, finish, grad)
    total_grad = wide(grad.total)
    new_weight = refresh(weight, total_grad[:F], second_weight)
    new_bias = refresh(bias, total_grad[F], second_bias)
    return (activations, grad_features.reshape(-1, F), new_weight, new_bias)


def solution(mesh):
    fine = Mesh(mesh.devices.reshape(Z, 2, 4, 4), ("z", "core", "y", "x"))
    row = ("z", "core")
    col = ("y", "x")
    placed = (
        P(col + row, None),
        P(row, col, None, None, None),
        P(row, col, None),
        P(row, col, None),
        P(row, col),
        P(),
        P(),
        P(),
        P(),
        P(row + col, None),
    )
    return jax.shard_map(
        per_device,
        mesh=fine,
        in_specs=placed,
        out_specs=(P(row + col, None), P(col + row, None), P(), P()),
        check_vma=False,
    )
```

```python
import functools

import jax
import jax.numpy as jnp
from jax import lax
from jax.experimental import pallas as pl
from jax.experimental.pallas import tpu as pltpu
from jax.sharding import Mesh, PartitionSpec as P

learn_rate = 0.1
TILE = 128
F = 512
BLOCK_TILES = 32
UNROLL = 4
Z = 8
VMEM_BYTES = 28 * 1024 * 1024


def refresh(param, grad, second):
    moment = 0.9 * second + 0.1 * grad * grad
    return param - learn_rate * grad / (jnp.sqrt(moment) + 1e-06)


def select(index, table):
    return jnp.take(jnp.array(table, jnp.int32), index)


def pick(index, other, same_table, other_table):
    return jnp.where(other == 0, select(index, same_table), select(index, other_table))


def row_tile_parts(t):
    dy = (t // 8 - lax.axis_index("y")) % 4
    dx = (t // 2 % 4 - lax.axis_index("x")) % 4
    x_first = lax.axis_index("core") == 0
    return jnp.where(x_first, dx, dy), jnp.where(x_first, dy, dx), t % 2


def scatter_xy_place(t):
    first, second, half = row_tile_parts(t)
    return select(first, [3, 1, 0, 2]) * 8 + second * 2 + half


def gather_xy_place(t):
    first, second, half = row_tile_parts(t)
    order = [0, 2, 3, 1]
    return select(second, order) * 8 + select(first, order) * 2 + half


def col_tile_parts(t):
    dz = (t // 4 - lax.axis_index("z")) % Z
    core = lax.axis_index("core")
    return dz, core, (t // 2 % 2 != core).astype(jnp.int32), t % 2


def gather_z_place(t):
    dz, core, other, half = col_tile_parts(t)
    behind = jnp.where(core == 0, (Z - dz) % Z, dz)
    return pick(behind, other, [0, 4, 8, 12, 16, 28, 24, 20], [2, 6, 10, 14, 30, 26, 22, 18]) + half


def scatter_z_place(t):
    dz, core, other, half = col_tile_parts(t)
    ahead = jnp.where(core == 0, dz, (Z - dz) % Z)
    return pick(ahead, other, [30, 28, 24, 10, 8, 4, 6, 18], [22, 26, 14, 12, 0, 2, 16, 20]) + half


def slot_order(first):
    index = jnp.arange(first.shape[0], dtype=jnp.int32)
    later = (~first).astype(jnp.int32)
    key = later * first.shape[0] + index
    rank = jnp.sum((key[None, :] < key[:, None]).astype(jnp.int32), axis=1)
    return jnp.sum(jnp.where(rank[None, :] == index[:, None], index[None, :], 0), axis=1)


def slot_loop(start, stop, order, sources, targets, base, values, panel, acc, flip):
    contract = ((0,), (0,)) if flip else ((1,), (0,))
    spare = acc.shape[0] - 1
    last = values.shape[0] - 1

    def step(group, carry):
        for part in range(UNROLL):
            i = start + group * UNROLL + part
            k = order[jnp.minimum(i, last)]
            source = sources[k]
            target = jnp.where(i < stop, targets[k] - base, spare)
            for column in range(0, F, 256):
                columns = slice(column, column + 256)
                acc[target, :, columns] += lax.dot_general(
                    values[k],
                    panel[source, :, columns],
                    (contract, ((), ())),
                    preferred_element_type=jnp.float32,
                )
        return carry

    lax.fori_loop(0, (stop - start + UNROLL - 1) // UNROLL, step, 0)


def write_out(acc, outs):
    start = 0
    for out in outs:
        for t in range(out.shape[0]):
            out[t] = acc[start + t].astype(out.dtype)
        start += out.shape[0]


def first_kernel(flip, n_panels, order, sources, targets, counts, values, *refs):
    panels, refs = refs[:n_panels], refs[n_panels:]
    copies = []
    if flip:
        outs, panel, fetched, acc, sems = refs[:-4], refs[-4], refs[-3], refs[-2], refs[-1]
        copies.append(pltpu.make_async_copy(values, fetched, sems.at[n_panels]))
        values = fetched
    else:
        outs, panel, acc, sems = refs[:-3], refs[-3], refs[-2], refs[-1]
    start = 0
    for i, piece in enumerate(panels):
        tiles = piece.shape[0]
        copies.append(pltpu.make_async_copy(piece, panel.at[pl.ds(start, tiles)], sems.at[i]))
        start += tiles
    for copy in copies:
        copy.start()
    acc[...] = jnp.zeros_like(acc)
    for copy in copies:
        copy.wait()
    slot_loop(0, counts[0], order, sources, targets, 0, values, panel, acc, flip)
    write_out(acc, outs)


def second_kernel(flip, base, order, sources, targets, counts, values, panel, *refs):
    outs, acc = refs[:-1], refs[-1]
    acc[...] = jnp.zeros_like(acc)
    slot_loop(counts[0], counts[1], order, sources, targets, base, values, panel, acc, flip)
    write_out(acc, outs)


def product_calls(flip, sources, targets, count, values, panels, first_tiles, second_tiles):
    hbm = pl.BlockSpec(memory_space=pl.ANY)
    in_hbm = pl.BlockSpec(memory_space=pltpu.HBM)
    smem = pl.BlockSpec(memory_space=pltpu.SMEM)
    vmem = pl.BlockSpec(memory_space=pltpu.VMEM)
    slots = values.shape[0]
    base = sum(first_tiles)
    is_first = (targets < base) & (jnp.arange(slots) < count)
    scalars = (
        slot_order(is_first),
        sources,
        targets,
        jnp.stack([jnp.sum(is_first, dtype=jnp.int32), count]),
    )
    params = pltpu.CompilerParams(vmem_limit_bytes=VMEM_BYTES)
    cost = pl.CostEstimate(
        flops=4 * slots * TILE * TILE * F, bytes_accessed=16 * 2**20, transcendentals=0
    )

    def tiles_of(counts, last=jnp.bfloat16):
        dtypes = [jnp.bfloat16] * (len(counts) - 1) + [last]
        return [jax.ShapeDtypeStruct((n, TILE, F), d) for n, d in zip(counts, dtypes)]

    fetched = [jax.ShapeDtypeStruct(values.shape, values.dtype)] if flip else []
    outs = pl.pallas_call(
        functools.partial(first_kernel, flip, len(panels)),
        out_shape=tiles_of(first_tiles + [BLOCK_TILES]) + fetched,
        in_specs=[smem] * 4 + [in_hbm if flip else vmem] + [hbm] * len(panels),
        out_specs=[vmem] * (len(first_tiles) + 1 + len(fetched)),
        scratch_shapes=[
            pltpu.VMEM((base + 1, TILE, F), jnp.float32),
            pltpu.SemaphoreType.DMA((len(panels) + 1,)),
        ],
        compiler_params=params,
        cost_estimate=cost,
    )(*scalars, values, *panels)

    first, panel = outs[: len(first_tiles)], outs[len(first_tiles)]
    if flip:
        values = outs[-1]

    def finish(panel):
        return pl.pallas_call(
            functools.partial(second_kernel, flip, base),
            out_shape=tiles_of(second_tiles, jnp.bfloat16 if flip else jnp.float32),
            in_specs=[smem] * 4 + [vmem] * 2,
            out_specs=[vmem] * len(second_tiles),
            scratch_shapes=[pltpu.VMEM((BLOCK_TILES - base + 1, TILE, F), jnp.float32)],
            compiler_params=params,
            cost_estimate=cost,
        )(*scalars, values, panel)

    return first, panel, finish


def dense_kernel(
    aggregated, cotangent, low_weight, bias, activations, grad_pre, grad_aggregated
):
    w = low_weight[...]
    pre = jnp.dot(aggregated[...], w, preferred_element_type=jnp.float32) + bias[...]
    sigma = jax.nn.sigmoid(pre)
    grad = cotangent[...].astype(jnp.float32) * sigma * (1.0 + pre * (1.0 - sigma))
    low_grad = grad.astype(jnp.bfloat16)
    activations[...] = (pre * sigma).astype(jnp.bfloat16)
    grad_pre[...] = low_grad
    grad_aggregated[...] = lax.dot_general(
        low_grad, w, (((1,), (1,)), ((), ())), preferred_element_type=jnp.float32
    ).astype(jnp.bfloat16)


def dense_call(aggregated, cotangent, low_weight, bias):
    shape = jax.ShapeDtypeStruct(aggregated.shape, jnp.bfloat16)
    return pl.pallas_call(
        dense_kernel,
        out_shape=[shape] * 3,
        compiler_params=pltpu.CompilerParams(vmem_limit_bytes=VMEM_BYTES),
    )(aggregated, cotangent, low_weight, bias)


def swap(value, axis, bit):
    size = lax.axis_size(axis)
    return lax.ppermute(value, axis, [(i, i ^ (1 << bit)) for i in range(size)])


def shift(value, axes, by):
    pairs = []
    for core, axis in enumerate(axes):
        for y in range(4):
            for x in range(4):
                to = (y, (x + by) % 4) if axis == "x" else ((y + by) % 4, x)
                pairs.append((core * 16 + y * 4 + x, core * 16 + to[0] * 4 + to[1]))
    return lax.ppermute(value, ("core", "y", "x"), pairs)


def advance(value):
    pairs = []
    for z in range(Z):
        pairs += [(z * 2, (z + 1) % Z * 2), (z * 2 + 1, (z - 1) % Z * 2 + 1)]
    return lax.ppermute(value, ("z", "core"), pairs)


def wide(value):
    return value.astype(jnp.float32)


def low(value):
    return value.astype(jnp.bfloat16)


def join(*values):
    return jnp.concatenate(values, axis=0)


def gather_z(features):
    own = features.reshape(2, TILE, F)
    a1 = advance(own)
    other = swap(own, "core", 0)
    b1 = advance(other)
    a2 = advance(a1)
    b2 = advance(b1)
    a3 = advance(a2)
    b3 = advance(b2)
    near, a4 = lax.optimization_barrier((join(a1, b1, a2, b2), advance(a3)))
    pieces = [own, other, a1, b1, a2, b2, a3, b3, a4]
    return pieces + [swap(near, "core", 0), swap(join(a3, b3, a4), "core", 0)]


def scatter_xy(far_up, far_down, up_a, up_b, down_a, down_b, own):
    axes = ("x", "y")
    from_below = shift(far_up, axes, 1)
    from_above = shift(far_down, axes, -1)
    below_b = shift(up_b, axes, 1)
    above_a = shift(down_a, axes, -1)
    below_a = shift(low(wide(up_a) + wide(from_below)), axes, 1)
    above_b = shift(low(wide(down_b) + wide(from_above)), axes, -1)
    sum_a = own[:4] + wide(below_a) + wide(above_a)
    sum_b = low(own[4:] + wide(below_b) + wide(above_b))
    axes = ("y", "x")
    below = shift(low(sum_a[2:]), axes, 1)
    above = shift(sum_b[2:], axes, -1)
    far = shift(sum_b[:2], axes, 2)
    return (sum_a[:2] + wide(far)) + (wide(below) + wide(above))


def gather_xy(own, grad):
    axes = ("x", "y")
    below, above, far = (shift(own, axes, by) for by in (1, -1, 2))
    grad.halve("core", 0)
    axes = ("y", "x")
    first = grad.beside(join(own, below))
    above_first, below_first = shift(first, axes, -1), shift(first, axes, 1)
    grad.halve("z", 0)
    last = grad.beside(join(above, far))
    below_last, above_last = shift(last, axes, 1), shift(last, axes, -1)
    grad.halve("z", 1)
    above_first, below_last = grad.beside((above_first, below_last))
    far = [shift(above_first, axes, -1), shift(below_last, axes, 1)]
    grad.halve("z", 2)
    grad.double("x", 0)
    panels = grad.beside([first, last, below_first, below_last, above_first, above_last] + far)
    grad.double("x", 1)
    return panels


class GradSum:
    def __init__(self, local):
        self.total = local

    def beside(self, message):
        self.total, message = lax.optimization_barrier((self.total, message))
        return message

    def halve(self, axis, bit):
        side = lax.axis_index(axis) >> bit & 1
        rows = self.total.shape[0] // 2
        keep = lax.dynamic_slice_in_dim(self.total, side * rows, rows, 0)
        send = lax.dynamic_slice_in_dim(self.total, (1 - side) * rows, rows, 0)
        message = send if axis == "core" else low(send)
        self.total = keep + wide(swap(message, axis, bit))

    def double(self, axis, bit):
        self.total = self.total + swap(self.total, axis, bit)

    def regather(self, axis, bit):
        self.total = low(self.total)
        side = lax.axis_index(axis) >> bit & 1
        other = swap(self.total, axis, bit)
        self.total = join(
            jnp.where(side == 0, self.total, other), jnp.where(side == 0, other, self.total)
        )


def scatter_z(other_first, own_first, panel, finish, grad):
    first = swap(grad.beside(other_first), "core", 0)
    grad.double("y", 0)

    def term(a, b, start):
        return wide(a[start : start + 2]) + wide(b[start : start + 2])

    a, b, panel = grad.beside(
        (low(term(own_first, first, 0)), low(term(own_first, first, 4)), panel)
    )
    a, b = advance(a), advance(b)
    grad.double("y", 1)
    other_next, other_last, own_next, own_last = finish(panel)
    near = swap(other_next, "core", 0)
    last = swap(other_last, "core", 0)
    a = advance(grad.beside(low(term(own_first, first, 2) + wide(a))))
    grad.regather("z", 2)
    b = advance(low(term(own_first, first, 6) + wide(b)))
    a = advance(grad.beside(low(term(own_next, near, 0) + wide(a))))
    grad.regather("z", 1)
    b = advance(low(term(own_next, near, 2) + wide(b)))
    a = advance(grad.beside(low(term(own_last, last, 0) + wide(a))))
    grad.regather("z", 0)
    b = swap(grad.beside(b), "core", 0)
    grad.regather("core", 0)
    return low(term(own_last, last, 2) + wide(a) + wide(b))


def per_device(
    features,
    tile_values,
    tile_row,
    tile_col,
    tile_count,
    weight,
    bias,
    second_weight,
    second_bias,
    cotangent,
):
    values = tile_values[0, 0]
    rows_local = tile_row[0, 0]
    cols_local = tile_col[0, 0]
    count = tile_count[0, 0]
    low_weight = weight.astype(jnp.bfloat16)

    first, panel, finish = product_calls(
        False,
        gather_z_place(cols_local),
        scatter_xy_place(rows_local),
        count,
        values,
        gather_z(features),
        [4, 4],
        [4, 4, 4, 4, 8],
    )
    aggregated = low(scatter_xy(*first, *finish(panel))).reshape(-1, F)
    activations, grad_pre, grad_aggregated = dense_call(
        aggregated, cotangent, low_weight, bias.reshape(1, F)
    )

    with_ones = jnp.concatenate(
        [aggregated, jnp.ones((aggregated.shape[0], TILE), jnp.bfloat16)], axis=1
    )
    local_grad = lax.dot_general(
        with_ones, grad_pre, (((0,), (0,)), ((), ())), preferred_element_type=jnp.float32
    )
    grad = GradSum(local_grad)
    grad_panels = gather_xy(grad_aggregated.reshape(-1, TILE, F), grad)

    first, panel, finish = product_calls(
        True,
        gather_xy_place(rows_local),
        scatter_z_place(cols_local),
        count,
        values,
        grad_panels,
        [8, 8],
        [4, 4, 4, 4],
    )
    grad_features = scatter_z(*first, panel, finish, grad)
    total_grad = wide(grad.total)
    new_weight = refresh(weight, total_grad[:F], second_weight)
    new_bias = refresh(bias, total_grad[F], second_bias)
    return (activations, grad_features.reshape(-1, F), new_weight, new_bias)


def solution(mesh):
    fine = Mesh(mesh.devices.reshape(Z, 2, 4, 4), ("z", "core", "y", "x"))
    row = ("z", "core")
    col = ("y", "x")
    placed = (
        P(col + row, None),
        P(row, col, None, None, None),
        P(row, col, None),
        P(row, col, None),
        P(row, col),
        P(),
        P(),
        P(),
        P(),
        P(row + col, None),
    )
    return jax.shard_map(
        per_device,
        mesh=fine,
        in_specs=placed,
        out_specs=(P(row + col, None), P(col + row, None), P(), P()),
        check_vma=False,
    )
```

```python
import functools

import jax
import jax.numpy as jnp
from jax import lax
from jax.experimental import pallas as pl
from jax.experimental.pallas import tpu as pltpu
from jax.sharding import Mesh, PartitionSpec as P

learn_rate = 0.1
TILE = 128
F = 512
BLOCK_TILES = 32
UNROLL = 4
Z = 8
VMEM_BYTES = 20 * 1024 * 1024


def refresh(param, grad, second):
    moment = 0.9 * second + 0.1 * grad * grad
    return param - learn_rate * grad / (jnp.sqrt(moment) + 1e-06)


def select(index, table):
    return jnp.take(jnp.array(table, jnp.int32), index)


def pick(index, other, same_table, other_table):
    return jnp.where(other == 0, select(index, same_table), select(index, other_table))


def row_tile_parts(t):
    dy = (t // 8 - lax.axis_index("y")) % 4
    dx = (t // 2 % 4 - lax.axis_index("x")) % 4
    x_first = lax.axis_index("core") == 0
    return jnp.where(x_first, dx, dy), jnp.where(x_first, dy, dx), t % 2


def scatter_xy_place(t):
    first, second, half = row_tile_parts(t)
    return select(first, [3, 1, 0, 2]) * 8 + second * 2 + half


def gather_xy_place(t):
    first, second, half = row_tile_parts(t)
    order = [0, 2, 3, 1]
    return select(second, order) * 8 + select(first, order) * 2 + half


def col_tile_parts(t):
    dz = (t // 4 - lax.axis_index("z")) % Z
    core = lax.axis_index("core")
    return dz, core, (t // 2 % 2 != core).astype(jnp.int32), t % 2


def gather_z_place(t):
    dz, core, other, half = col_tile_parts(t)
    behind = jnp.where(core == 0, (Z - dz) % Z, dz)
    return pick(behind, other, [0, 4, 8, 12, 16, 28, 24, 20], [2, 6, 10, 14, 30, 26, 22, 18]) + half


def scatter_z_place(t):
    dz, core, other, half = col_tile_parts(t)
    ahead = jnp.where(core == 0, dz, (Z - dz) % Z)
    return pick(ahead, other, [30, 28, 24, 10, 8, 4, 6, 18], [22, 26, 14, 12, 0, 2, 16, 20]) + half


def slot_order(first):
    index = jnp.arange(first.shape[0], dtype=jnp.int32)
    later = (~first).astype(jnp.int32)
    key = later * first.shape[0] + index
    rank = jnp.sum((key[None, :] < key[:, None]).astype(jnp.int32), axis=1)
    return jnp.sum(jnp.where(rank[None, :] == index[:, None], index[None, :], 0), axis=1)


def slot_loop(start, stop, order, sources, targets, base, values, panel, acc, flip):
    contract = ((0,), (0,)) if flip else ((1,), (0,))
    spare = acc.shape[0] - 1
    last = values.shape[0] - 1

    def step(group, carry):
        for part in range(UNROLL):
            i = start + group * UNROLL + part
            k = order[jnp.minimum(i, last)]
            source = sources[k]
            target = jnp.where(i < stop, targets[k] - base, spare)
            for column in range(0, F, 256):
                columns = slice(column, column + 256)
                acc[target, :, columns] += lax.dot_general(
                    values[k],
                    panel[source, :, columns],
                    (contract, ((), ())),
                    preferred_element_type=jnp.float32,
                )
        return carry

    lax.fori_loop(0, (stop - start + UNROLL - 1) // UNROLL, step, 0)


def write_out(acc, outs):
    start = 0
    for out in outs:
        for t in range(out.shape[0]):
            out[t] = acc[start + t].astype(out.dtype)
        start += out.shape[0]


def first_kernel(flip, n_panels, order, sources, targets, counts, values, *refs):
    panels, refs = refs[:n_panels], refs[n_panels:]
    copies = []
    if flip:
        outs, panel, fetched, acc, sems = refs[:-4], refs[-4], refs[-3], refs[-2], refs[-1]
        copies.append(pltpu.make_async_copy(values, fetched, sems.at[n_panels]))
        values = fetched
    else:
        outs, panel, acc, sems = refs[:-3], refs[-3], refs[-2], refs[-1]
    start = 0
    for i, piece in enumerate(panels):
        tiles = piece.shape[0]
        copies.append(pltpu.make_async_copy(piece, panel.at[pl.ds(start, tiles)], sems.at[i]))
        start += tiles
    for copy in copies:
        copy.start()
    acc[...] = jnp.zeros_like(acc)
    for copy in copies:
        copy.wait()
    slot_loop(0, counts[0], order, sources, targets, 0, values, panel, acc, flip)
    write_out(acc, outs)


def second_kernel(flip, base, order, sources, targets, counts, values, panel, *refs):
    outs, acc = refs[:-1], refs[-1]
    acc[...] = jnp.zeros_like(acc)
    slot_loop(counts[0], counts[1], order, sources, targets, base, values, panel, acc, flip)
    write_out(acc, outs)


def product_calls(flip, sources, targets, count, values, panels, first_tiles, second_tiles):
    hbm = pl.BlockSpec(memory_space=pl.ANY)
    in_hbm = pl.BlockSpec(memory_space=pltpu.HBM)
    smem = pl.BlockSpec(memory_space=pltpu.SMEM)
    vmem = pl.BlockSpec(memory_space=pltpu.VMEM)
    slots = values.shape[0]
    base = sum(first_tiles)
    is_first = (targets < base) & (jnp.arange(slots) < count)
    scalars = (
        slot_order(is_first),
        sources,
        targets,
        jnp.stack([jnp.sum(is_first, dtype=jnp.int32), count]),
    )
    params = pltpu.CompilerParams(vmem_limit_bytes=VMEM_BYTES)
    cost = pl.CostEstimate(
        flops=4 * slots * TILE * TILE * F, bytes_accessed=16 * 2**20, transcendentals=0
    )

    def tiles_of(counts, last=jnp.bfloat16):
        dtypes = [jnp.bfloat16] * (len(counts) - 1) + [last]
        return [jax.ShapeDtypeStruct((n, TILE, F), d) for n, d in zip(counts, dtypes)]

    fetched = [jax.ShapeDtypeStruct(values.shape, values.dtype)] if flip else []
    outs = pl.pallas_call(
        functools.partial(first_kernel, flip, len(panels)),
        out_shape=tiles_of(first_tiles + [BLOCK_TILES]) + fetched,
        in_specs=[smem] * 4 + [in_hbm if flip else vmem] + [hbm] * len(panels),
        out_specs=[vmem] * (len(first_tiles) + 1 + len(fetched)),
        scratch_shapes=[
            pltpu.VMEM((base + 1, TILE, F), jnp.float32),
            pltpu.SemaphoreType.DMA((len(panels) + 1,)),
        ],
        compiler_params=params,
        cost_estimate=cost,
    )(*scalars, values, *panels)

    first, panel = outs[: len(first_tiles)], outs[len(first_tiles)]
    if flip:
        values = outs[-1]

    def finish(panel):
        return pl.pallas_call(
            functools.partial(second_kernel, flip, base),
            out_shape=tiles_of(second_tiles, jnp.bfloat16 if flip else jnp.float32),
            in_specs=[smem] * 4 + [vmem] * 2,
            out_specs=[vmem] * len(second_tiles),
            scratch_shapes=[pltpu.VMEM((BLOCK_TILES - base + 1, TILE, F), jnp.float32)],
            compiler_params=params,
            cost_estimate=cost,
        )(*scalars, values, panel)

    return first, panel, finish


def dense_kernel(
    aggregated, cotangent, low_weight, bias, activations, grad_pre, grad_aggregated
):
    w = low_weight[...]
    pre = jnp.dot(aggregated[...], w, preferred_element_type=jnp.float32) + bias[...]
    sigma = jax.nn.sigmoid(pre)
    grad = cotangent[...].astype(jnp.float32) * sigma * (1.0 + pre * (1.0 - sigma))
    low_grad = grad.astype(jnp.bfloat16)
    activations[...] = (pre * sigma).astype(jnp.bfloat16)
    grad_pre[...] = low_grad
    grad_aggregated[...] = lax.dot_general(
        low_grad, w, (((1,), (1,)), ((), ())), preferred_element_type=jnp.float32
    ).astype(jnp.bfloat16)


def dense_call(aggregated, cotangent, low_weight, bias):
    shape = jax.ShapeDtypeStruct(aggregated.shape, jnp.bfloat16)
    return pl.pallas_call(
        dense_kernel,
        out_shape=[shape] * 3,
        compiler_params=pltpu.CompilerParams(vmem_limit_bytes=VMEM_BYTES),
    )(aggregated, cotangent, low_weight, bias)


def swap(value, axis, bit):
    size = lax.axis_size(axis)
    return lax.ppermute(value, axis, [(i, i ^ (1 << bit)) for i in range(size)])


def shift(value, axes, by):
    pairs = []
    for core, axis in enumerate(axes):
        for y in range(4):
            for x in range(4):
                to = (y, (x + by) % 4) if axis == "x" else ((y + by) % 4, x)
                pairs.append((core * 16 + y * 4 + x, core * 16 + to[0] * 4 + to[1]))
    return lax.ppermute(value, ("core", "y", "x"), pairs)


def advance(value):
    pairs = []
    for z in range(Z):
        pairs += [(z * 2, (z + 1) % Z * 2), (z * 2 + 1, (z - 1) % Z * 2 + 1)]
    return lax.ppermute(value, ("z", "core"), pairs)


def wide(value):
    return value.astype(jnp.float32)


def low(value):
    return value.astype(jnp.bfloat16)


def join(*values):
    return jnp.concatenate(values, axis=0)


def gather_z(features):
    own = features.reshape(2, TILE, F)
    a1 = advance(own)
    other = swap(own, "core", 0)
    b1 = advance(other)
    a2 = advance(a1)
    b2 = advance(b1)
    a3 = advance(a2)
    b3 = advance(b2)
    near, a4 = lax.optimization_barrier((join(a1, b1, a2, b2), advance(a3)))
    pieces = [own, other, a1, b1, a2, b2, a3, b3, a4]
    return pieces + [swap(near, "core", 0), swap(join(a3, b3, a4), "core", 0)]


def scatter_xy(far_up, far_down, up_a, up_b, down_a, down_b, own):
    axes = ("x", "y")
    from_below = shift(far_up, axes, 1)
    from_above = shift(far_down, axes, -1)
    below_b = shift(up_b, axes, 1)
    above_a = shift(down_a, axes, -1)
    below_a = shift(low(wide(up_a) + wide(from_below)), axes, 1)
    above_b = shift(low(wide(down_b) + wide(from_above)), axes, -1)
    sum_a = own[:4] + wide(below_a) + wide(above_a)
    sum_b = low(own[4:] + wide(below_b) + wide(above_b))
    axes = ("y", "x")
    below = shift(low(sum_a[2:]), axes, 1)
    above = shift(sum_b[2:], axes, -1)
    far = shift(sum_b[:2], axes, 2)
    return (sum_a[:2] + wide(far)) + (wide(below) + wide(above))


def gather_xy(own, grad):
    axes = ("x", "y")
    below, above, far = (shift(own, axes, by) for by in (1, -1, 2))
    grad.halve("core", 0)
    axes = ("y", "x")
    first = grad.beside(join(own, below))
    above_first, below_first = shift(first, axes, -1), shift(first, axes, 1)
    grad.halve("z", 0)
    last = grad.beside(join(above, far))
    below_last, above_last = shift(last, axes, 1), shift(last, axes, -1)
    grad.halve("z", 1)
    above_first, below_last = grad.beside((above_first, below_last))
    far = [shift(above_first, axes, -1), shift(below_last, axes, 1)]
    grad.halve("z", 2)
    grad.double("x", 0)
    panels = grad.beside([first, last, below_first, below_last, above_first, above_last] + far)
    grad.double("x", 1)
    return panels


class GradSum:
    def __init__(self, local):
        self.total = local

    def after(self, message):
        self.total, _ = lax.optimization_barrier((self.total, message))

    def beside(self, message):
        self.total, message = lax.optimization_barrier((self.total, message))
        return message

    def halve(self, axis, bit):
        side = lax.axis_index(axis) >> bit & 1
        rows = self.total.shape[0] // 2
        keep = lax.dynamic_slice_in_dim(self.total, side * rows, rows, 0)
        send = lax.dynamic_slice_in_dim(self.total, (1 - side) * rows, rows, 0)
        message = send if axis == "core" else low(send)
        self.total = keep + wide(swap(message, axis, bit))

    def double(self, axis, bit):
        self.total = self.total + swap(self.total, axis, bit)

    def regather(self, axis, bit, arrived):
        self.total = low(self.total)
        side = lax.axis_index(axis) >> bit & 1
        other, _ = lax.optimization_barrier((swap(self.total, axis, bit), arrived))
        self.total = join(
            jnp.where(side == 0, self.total, other), jnp.where(side == 0, other, self.total)
        )


def scatter_z(other_first, own_first, panel, finish, grad):
    first = swap(grad.beside(other_first), "core", 0)
    grad.double("y", 0)

    def term(a, b, start):
        return wide(a[start : start + 2]) + wide(b[start : start + 2])

    a, b, panel = grad.beside(
        (low(term(own_first, first, 0)), low(term(own_first, first, 4)), panel)
    )
    a, b = advance(a), advance(b)
    grad.double("y", 1)
    other_next, other_last, own_next, own_last = finish(panel)
    near = swap(other_next, "core", 0)
    last = swap(other_last, "core", 0)
    a = low(term(own_first, first, 2) + wide(a))
    grad.after(a)
    a = advance(a)
    grad.regather("z", 2, a)
    b = advance(low(term(own_first, first, 6) + wide(b)))
    a = low(term(own_next, near, 0) + wide(a))
    grad.after(a)
    a = advance(a)
    grad.regather("z", 1, a)
    b = advance(low(term(own_next, near, 2) + wide(b)))
    a = low(term(own_last, last, 0) + wide(a))
    grad.after(a)
    a = advance(a)
    grad.regather("z", 0, a)
    grad.after(b)
    b = swap(b, "core", 0)
    grad.regather("core", 0, b)
    return low(term(own_last, last, 2) + wide(a) + wide(b))


def per_device(
    features,
    tile_values,
    tile_row,
    tile_col,
    tile_count,
    weight,
    bias,
    second_weight,
    second_bias,
    cotangent,
):
    values = tile_values[0, 0]
    rows_local = tile_row[0, 0]
    cols_local = tile_col[0, 0]
    count = tile_count[0, 0]
    low_weight = weight.astype(jnp.bfloat16)

    first, panel, finish = product_calls(
        False,
        gather_z_place(cols_local),
        scatter_xy_place(rows_local),
        count,
        values,
        gather_z(features),
        [4, 4],
        [4, 4, 4, 4, 8],
    )
    aggregated = low(scatter_xy(*first, *finish(panel))).reshape(-1, F)
    activations, grad_pre, grad_aggregated = dense_call(
        aggregated, cotangent, low_weight, bias.reshape(1, F)
    )

    with_ones = jnp.concatenate(
        [aggregated, jnp.ones((aggregated.shape[0], TILE), jnp.bfloat16)], axis=1
    )
    local_grad = lax.dot_general(
        with_ones, grad_pre, (((0,), (0,)), ((), ())), preferred_element_type=jnp.float32
    )
    grad = GradSum(local_grad)
    grad_panels = gather_xy(grad_aggregated.reshape(-1, TILE, F), grad)

    first, panel, finish = product_calls(
        True,
        gather_xy_place(rows_local),
        scatter_z_place(cols_local),
        count,
        values,
        grad_panels,
        [8, 8],
        [4, 4, 4, 4],
    )
    grad_features = scatter_z(*first, panel, finish, grad)
    total_grad = wide(grad.total)
    new_weight = refresh(weight, total_grad[:F], second_weight)
    new_bias = refresh(bias, total_grad[F], second_bias)
    return (activations, grad_features.reshape(-1, F), new_weight, new_bias)


def solution(mesh):
    fine = Mesh(mesh.devices.reshape(Z, 2, 4, 4), ("z", "core", "y", "x"))
    row = ("z", "core")
    col = ("y", "x")
    placed = (
        P(col + row, None),
        P(row, col, None, None, None),
        P(row, col, None),
        P(row, col, None),
        P(row, col),
        P(),
        P(),
        P(),
        P(),
        P(row + col, None),
    )
    return jax.shard_map(
        per_device,
        mesh=fine,
        in_specs=placed,
        out_specs=(P(row + col, None), P(col + row, None), P(), P()),
        check_vma=False,
    )
```
